512 devices in a mesh: blk: 128 (over y_hi, z, x), mp: 4 (over y_lo, core).
Axes of the slice: x: 4, y: 8 (y_hi: 4, y_lo: 2; y = y_hi * 2 + y_lo), z: 8, core: 2. Of those that a mesh axis runs over, the one named last changes fastest.
Arguments:
- queries: bfloat16 [1024, 32, 128], P(('blk', 'mp')), may hold values from -32 to 32
- passages: bfloat16 [1024, 180, 128], P(('blk', 'mp')), may hold values from -32 to 32
- lengths: int32 [1024], P(('blk', 'mp')), may hold values from 45 to 180
- pos_index: int32 [128, 8], P('blk'), may hold values from 0 to 7, each once within a row
Outputs:
- query_loss: float32 [1024], P(('blk', 'mp'))
- query_grads: float32 [1024, 32, 128], P(('blk', 'mp'))
- passage_grads: float32 [1024, 180, 128], P(('blk', 'mp'))
The draws below stay inside these ranges and needn't reach their ends.
Inputs may be any that keep to these rules, and one draw needn't show every extreme that they name: Each row of pos_index holds every number of 0 to 7 once.
All inputs are finite; a program needn't handle non-finite values.
Results may differ from the reference program's by a relative error of at most 0.0035.
Values may be sent and summed in bfloat16 or wider, within the bound.
A program may use at most 64 MiB of HBM per device.

```python
import jax
import jax.numpy as jnp
from jax import lax

DIM = 128
QTOK = 32
PTOK = 180
WINDOW = 4
BLOCK_PAIRS = 8
BLOCKS = 128
PAIRS = 1024


def draw_queries(key, part):
    key = jax.random.fold_in(key, 11)
    values_drawn = 1.5 * jnp.clip(jax.random.normal(key, (PAIRS, QTOK, DIM), jnp.float32), -4.0, 4.0)
    return values_drawn.astype(jnp.bfloat16)


def draw_passages(key, part):
    key = jax.random.fold_in(key, 23)
    values_drawn = jnp.clip(jax.random.normal(key, (PAIRS, PTOK, DIM), jnp.float32), -4.0, 4.0)
    return values_drawn.astype(jnp.bfloat16)


def place_ends(values, rng, least, top_value):
    longest = values.shape.index(max(values.shape))
    spots = []
    for shift in (0, 1):
        where = [jax.random.randint(jax.random.fold_in(rng, axis), (), 0, length) for axis, length in enumerate(values.shape)]
        where[longest] = (where[longest] + shift) % values.shape[longest]
        spots.append(tuple(where))
    return values.at[spots[0]].set(least).at[spots[1]].set(top_value)


def setup_inputs(seed: int = 0) -> dict:
    splits = jax.random.split(jax.random.key(seed), 5)
    queries = draw_queries(jax.random.fold_in(splits[4], 71), 0)
    passages = draw_passages(jax.random.fold_in(splits[4], 71), 0)
    lengths = place_ends(jax.random.randint(splits[2], (PAIRS,), PTOK // 4, PTOK + 1), jax.random.fold_in(splits[2], 1), PTOK // 4, PTOK).astype(jnp.int32)
    pos_index = jax.vmap(lambda own: jax.random.permutation(own, BLOCK_PAIRS))(jax.random.split(splits[3], BLOCKS)).reshape((BLOCKS, BLOCK_PAIRS)).astype(jnp.int32)
    return {"queries": queries, "passages": passages, "lengths": lengths, "pos_index": pos_index}


NEG = -1e30


def block_terms(query_blk, pass_blk, len_blk, inv_root):
    n_query = query_blk.shape[0]
    n_pass = pass_blk.shape[0]
    logits = jnp.dot(query_blk.reshape(n_query * QTOK, DIM), pass_blk.reshape(n_pass * PTOK, DIM).T,
                     preferred_element_type=jnp.float32) * inv_root
    logits = logits.reshape(n_query, QTOK, n_pass, PTOK)
    usable = jnp.arange(PTOK)[None, :] < len_blk[:, None]
    masked = jnp.where(usable[None, None], logits, NEG)
    maximum = jnp.max(masked, axis=3)
    exp_terms = jnp.where(usable[None, None], jnp.exp(masked - maximum[..., None]), 0.0)
    sums_exp = jnp.sum(exp_terms, axis=3)
    log_length = jnp.log(len_blk.astype(jnp.float32))
    scores = jnp.sum(maximum + jnp.log(sums_exp) - log_length[None, None, :], axis=1)
    return scores, exp_terms, sums_exp


def reference(queries, passages, lengths, pos_index):
    inv_root = DIM ** -0.5
    query_blocks = queries.reshape(BLOCKS, BLOCK_PAIRS, QTOK, DIM)
    pass_blocks = passages.reshape(BLOCKS, BLOCK_PAIRS, PTOK, DIM)
    len_blocks = lengths.reshape(BLOCKS, BLOCK_PAIRS)

    def forward_one(operands):
        return block_terms(operands[0], operands[1], operands[2], inv_root)[0]

    all_scores = []
    for cycle_step in range(WINDOW):
        rolled_pass = jnp.roll(pass_blocks, -cycle_step, axis=0)
        rolled_len = jnp.roll(len_blocks, -cycle_step, axis=0)
        all_scores.append(lax.map(forward_one, (query_blocks, rolled_pass, rolled_len)))
    all_scores = jnp.stack(all_scores)
    maximum = jnp.max(all_scores, axis=(0, 3))
    row_lse = maximum + jnp.log(jnp.sum(jnp.exp(all_scores - maximum[None, :, :, None]), axis=(0, 3)))
    positive = (jnp.arange(BLOCK_PAIRS)[None, None, :] == pos_index[:, :, None]).astype(jnp.float32)
    pos_score = jnp.sum(all_scores[0] * positive, axis=-1)
    query_loss = (row_lse - pos_score).reshape(PAIRS)

    def backward_one(operands):
        query_blk, pass_blk, len_blk, coef = operands
        scores, exp_terms, sums_exp = block_terms(query_blk, pass_blk, len_blk, inv_root)
        weights = exp_terms / sums_exp[..., None]
        dlogit = (coef[:, None, :, None] * weights).astype(jnp.bfloat16)
        dlogit = dlogit.reshape(BLOCK_PAIRS * QTOK, BLOCK_PAIRS * PTOK)
        query_grad = jnp.dot(dlogit, pass_blk.reshape(BLOCK_PAIRS * PTOK, DIM),
                             preferred_element_type=jnp.float32) * inv_root
        pass_grad = jnp.dot(dlogit.T, query_blk.reshape(BLOCK_PAIRS * QTOK, DIM),
                            preferred_element_type=jnp.float32) * inv_root
        return query_grad.reshape(BLOCK_PAIRS, QTOK, DIM), pass_grad.reshape(BLOCK_PAIRS, PTOK, DIM)

    query_total = jnp.zeros((BLOCKS, BLOCK_PAIRS, QTOK, DIM), jnp.float32)
    pass_total = jnp.zeros((BLOCKS, BLOCK_PAIRS, PTOK, DIM), jnp.float32)
    for cycle_step in range(WINDOW):
        coef = jnp.exp(all_scores[cycle_step] - row_lse[:, :, None])
        if cycle_step == 0:
            coef = coef - positive
        rolled_pass = jnp.roll(pass_blocks, -cycle_step, axis=0)
        rolled_len = jnp.roll(len_blocks, -cycle_step, axis=0)
        query_grad, pass_grad = lax.map(backward_one, (query_blocks, rolled_pass, rolled_len, coef))
        query_total = query_total + query_grad
        pass_total = pass_total + jnp.roll(pass_grad, cycle_step, axis=0)
    return (query_loss, query_total.reshape(PAIRS, QTOK, DIM), pass_total.reshape(PAIRS, PTOK, DIM))
```

```python
import functools
import math

import jax
import jax.numpy as jnp
from jax import lax
from jax.experimental import pallas as pl
from jax.experimental.pallas import tpu as pltpu
from jax.sharding import PartitionSpec as P

WINDOW = 4
MP = 4
PER = 2
QTOK = 32
PTOK = 180
DIM = 128
ROWS = PER * PTOK
OWN = PER * QTOK
BLK = MP * OWN
SPAN = 2 * WINDOW - 1
NEG = -1e30
ROOT = DIM ** (-0.5)
MESH = pl.DeviceIdType.MESH
F32 = jnp.float32
BF16 = jnp.bfloat16


def spread_pairs(x):
    x = x + pltpu.roll(x, 4, 0)
    return x + pltpu.roll(x, 2, 0)


def max_pairs(x):
    x = jnp.maximum(x, pltpu.roll(x, 4, 0))
    return jnp.maximum(x, pltpu.roll(x, 2, 0))


def token_sum(x, same):
    hi = x.astype(BF16)
    rest = x - hi.astype(F32)
    mid = rest.astype(BF16)
    low = (rest - mid.astype(F32)).astype(BF16)
    dot = functools.partial(jnp.dot, preferred_element_type=F32)
    return dot(hi, same) + (dot(mid, same) + dot(low, same))


def work(
    blocks,
    q_hbm,
    p_hbm,
    len_ref,
    pos_ref,
    loss_ref,
    qg_ref,
    pg_ref,
    qall,
    p_ref,
    pcat,
    w_ref,
    gsend,
    grecv,
    sall,
    ctok,
    q_send,
    q_recv,
    s_send,
    s_recv,
    g_send,
    g_recv,
    local,
):
    b = lax.axis_index("blk")
    m = lax.axis_index("mp")

    def block(d):
        return lax.rem(b + (d + blocks), blocks)

    def lane(k):
        return lax.rem(m + k, MP)

    def remote(src, dst, send, recv, d, k):
        return pltpu.make_async_remote_copy(
            src_ref=src,
            dst_ref=dst,
            send_sem=send,
            recv_sem=recv,
            device_id={"blk": block(d), "mp": lane(k)},
            device_id_type=MESH,
        )

    barrier = pltpu.get_barrier_semaphore()
    near = [
        (d, k)
        for d in (3, 2, 1, -1, -2, -3, 0)
        for k in range(MP)
        if not (d == 0 and k == 0)
    ]
    for d, k in near:
        pl.semaphore_signal(
            barrier, inc=1, device_id={"blk": block(d), "mp": lane(k)}, device_id_type=MESH
        )
    own_q = pltpu.make_async_copy(q_hbm, qall.at[m], local.at[0])
    own_q.start()
    own_p = pltpu.make_async_copy(p_hbm, p_ref, local.at[1])
    own_p.start()

    row8 = lax.broadcasted_iota(jnp.int32, (8, BLK), 0)
    lane8 = lax.broadcasted_iota(jnp.int32, (8, BLK), 1)
    parity = row8 % 2
    group = row8 // 2
    lens = jnp.where(parity == 0, len_ref[0], len_ref[1])
    log_len = jnp.log(lens.astype(F32)) * QTOK
    query_of = lane8 // QTOK
    pos = jnp.zeros((8, BLK), jnp.int32)
    for n in range(MP * PER):
        pos = jnp.where(query_of == n, pos_ref[0, n], pos)
    same = (
        lax.broadcasted_iota(jnp.int32, (BLK, BLK), 0) // QTOK
        == lax.broadcasted_iota(jnp.int32, (BLK, BLK), 1) // QTOK
    ).astype(F32).astype(BF16)

    pl.semaphore_wait(barrier, len(near))
    waits = []
    for s in (3, 2, 1, 0):
        for k in range(MP):
            if s == 0 and k == 0:
                continue
            c = remote(
                q_hbm, qall.at[s * MP + m], q_send.at[s * MP + k], q_recv.at[s * MP + m], s, k
            )
            c.start()
            waits.append(c)

    own_p.wait()
    p_rows = p_ref[...]
    p32 = p_rows.astype(F32)
    odd = lax.broadcasted_iota(jnp.int32, (ROWS, DIM), 0) % 2
    pcat[:, :DIM] = jnp.where(odd == 0, p32, 0.0).astype(BF16)
    pcat[:, DIM:] = jnp.where(odd == 1, p32, 0.0).astype(BF16)
    token = (
        lax.broadcasted_iota(jnp.int32, (ROWS // 8, 8, BLK), 0) * 4
        + lax.broadcasted_iota(jnp.int32, (ROWS // 8, 8, BLK), 1) // 2
    )
    live = token < lens[None]

    own_q.wait()
    message = jnp.zeros((8, BLK), F32)
    for s in range(WINDOW):
        for k in range(MP):
            if s == 0 and k == 0:
                continue
            i = s * MP + lane(k)
            remote(q_hbm, qall.at[i], q_send.at[0], q_recv.at[i], s, k).wait_recv()
        q_blk = qall[s * MP : (s + 1) * MP].reshape(BLK, DIM)
        logits = lax.dot_general(
            p_rows, q_blk, (((1,), (1,)), ((), ())), preferred_element_type=F32
        ).reshape(ROWS // 8, 8, BLK)
        logits = jnp.where(live, logits, NEG)
        top = max_pairs(jnp.max(logits, axis=0))
        terms = jnp.exp2((logits - top[None]) * (ROOT * math.log2(math.e)))
        total = spread_pairs(jnp.sum(terms, axis=0))
        w_ref[s] = (terms * (1.0 / total)[None]).reshape(ROWS, BLK)
        score = token_sum(top * ROOT + jnp.log(total), same) - log_len
        message = jnp.where(group == s, score, message)

    sall[(WINDOW - 1) * MP + m] = message
    mine = (WINDOW - 1) * MP + m
    for d in (3, -3, 2, -2, 1, -1, 0):
        for k in range(MP):
            if d == 0 and k == 0:
                continue
            i = (WINDOW - 1 - d) * MP + m
            c = remote(
                sall.at[mine],
                sall.at[i],
                s_send.at[(d + WINDOW - 1) * MP + k],
                s_recv.at[i],
                d,
                k,
            )
            c.start()
            waits.append(c)

    for s in range(WINDOW):
        w = w_ref[s]
        hi = w.astype(BF16)
        low = (w - hi.astype(F32)).astype(BF16)
        over_rows = functools.partial(
            lax.dot_general,
            dimension_numbers=(((0,), (0,)), ((), ())),
            preferred_element_type=F32,
        )
        g = over_rows(hi, pcat[...]) + over_rows(low, pcat[...])
        gsend[s] = g.astype(BF16).reshape(MP, OWN, PER * DIM)
        for k in range(MP):
            if s == 0 and k == 0:
                continue
            c = remote(
                gsend.at[s, lane(k)],
                grecv.at[s * MP + m],
                g_send.at[s * MP + k],
                g_recv.at[s * MP + m],
                -s,
                k,
            )
            c.start()
            waits.append(c)
    grecv[m] = gsend[0, m]

    for d in range(1 - WINDOW, WINDOW):
        for k in range(MP):
            if d == 0 and k == 0:
                continue
            i = (d + WINDOW - 1) * MP + lane(k)
            remote(sall.at[mine], sall.at[i], s_send.at[0], s_recv.at[i], 0, k).wait_recv()

    tops = []
    for d in range(1 - WINDOW, WINDOW):
        t = jnp.max(sall[(d + WINDOW - 1) * MP : (d + WINDOW) * MP], axis=0)
        t = pltpu.roll(t, (-2 * d) % 8, 0) if d else t
        tops.append(jnp.where((group + d >= 0) & (group + d < WINDOW), t, NEG))
    top = functools.reduce(jnp.maximum, tops)
    top = jnp.maximum(
        top, jnp.where(parity == 0, pltpu.roll(top, 7, 0), pltpu.roll(top, 1, 0))
    )
    total = jnp.zeros((8, BLK), F32)
    for d in range(1 - WINDOW, WINDOW):
        there = pltpu.roll(top, (2 * d) % 8, 0) if d else top
        inside = (group - d >= 0) & (group - d < WINDOW)
        tile = sall[(d + WINDOW - 1) * MP : (d + WINDOW) * MP]
        t = jnp.sum(jnp.exp(jnp.where(inside[None], tile - there[None], NEG)), axis=0)
        total = total + (pltpu.roll(t, (-2 * d) % 8, 0) if d else t)
    total = total + jnp.where(
        parity == 0, pltpu.roll(total, 7, 0), pltpu.roll(total, 1, 0)
    )
    lse = top + jnp.log(total)

    first = group == 0
    hit = jnp.where(first & (pos == PER * m + parity), 1.0, 0.0)
    coef = jnp.exp(sall[mine] - lse) - hit
    pg = jnp.zeros((ROWS, DIM), F32)
    for s in range(WINDOW):
        c = spread_pairs(jnp.where(group == s, coef, 0.0))
        d_rows = (w_ref[s].reshape(ROWS // 8, 8, BLK) * c[None]).reshape(ROWS, BLK)
        q_blk = qall[s * MP : (s + 1) * MP].reshape(BLK, DIM)
        pg = pg + jnp.dot(d_rows.astype(BF16), q_blk, preferred_element_type=F32)
    pg_ref[...] = pg * ROOT

    lse_own = jnp.broadcast_to(lse[0:1], (8, BLK))
    found = jnp.zeros((8, BLK), F32)
    parts = []
    for k in range(MP):
        t = jnp.zeros((8, BLK), F32)
        for d in range(WINDOW):
            t = jnp.where(group == d, sall[(d + WINDOW - 1) * MP + k], t)
        here = first & (pos == PER * k + parity)
        found = jnp.where(here, t, found)
        parts.append(jnp.exp(t - lse_own) - jnp.where(here, 1.0, 0.0))
    parts.append(jnp.zeros((DIM - 8 * MP, BLK), F32))
    ctok[...] = jnp.concatenate(parts, axis=0).T
    loss = lse_own - jnp.broadcast_to(jnp.sum(found, axis=0, keepdims=True), (8, BLK))
    one = [
        jnp.sum(jnp.where(lane8[0:1] == m * OWN + n * QTOK, loss[0:1], 0.0)) for n in range(PER)
    ]
    place = lax.broadcasted_iota(jnp.int32, (1, PER), 1)
    loss_ref[...] = jnp.where(place == 0, one[0], one[1])

    for s in range(WINDOW):
        for k in range(MP):
            if s == 0 and k == 0:
                continue
            i = s * MP + lane(k)
            remote(gsend.at[0, 0], grecv.at[i], g_send.at[0], g_recv.at[i], 0, k).wait_recv()
    mine_tok = ctok[pl.ds(pl.multiple_of(m * OWN, OWN), OWN), :]
    qg = jnp.zeros((OWN, DIM), F32)
    for k in range(MP):
        for s in range(WINDOW):
            for p in range(PER):
                col = 8 * k + 2 * s + p
                g = grecv[s * MP + k, :, p * DIM : (p + 1) * DIM].astype(F32)
                qg = qg + mine_tok[:, col : col + 1] * g
    qg_ref[...] = qg * ROOT
    for c in waits:
        c.wait_send()


def store(loss_ref, qg_ref, pg_ref, loss_out, qg_out, pg_out, sems):
    copies = [
        pltpu.make_async_copy(src, dst, sems.at[i])
        for i, (src, dst) in enumerate(
            ((pg_ref, pg_out), (qg_ref, qg_out), (loss_ref, loss_out))
        )
    ]
    for c in copies:
        c.start()
    for c in copies:
        c.wait()


def on_device(blocks, queries, passages, lengths, pos_index):
    hbm = pl.BlockSpec(memory_space=pl.ANY)
    vmem = pl.BlockSpec(memory_space=pltpu.VMEM)
    smem = pl.BlockSpec(memory_space=pltpu.SMEM)
    shapes = ((1, PER), (OWN, DIM), (ROWS, DIM))
    slots = WINDOW * MP
    dma = pltpu.SemaphoreType.DMA
    results = pl.pallas_call(
        functools.partial(work, blocks),
        out_shape=tuple(pltpu.VMEM(s, F32) for s in shapes),
        in_specs=[hbm, hbm, smem, smem],
        out_specs=(vmem,) * 3,
        scratch_shapes=[
            pltpu.VMEM((slots, OWN, DIM), BF16),
            pltpu.VMEM((ROWS, DIM), BF16),
            pltpu.VMEM((ROWS, PER * DIM), BF16),
            pltpu.VMEM((WINDOW, ROWS, BLK), F32),
            pltpu.VMEM((WINDOW, MP, OWN, PER * DIM), BF16),
            pltpu.VMEM((slots, OWN, PER * DIM), BF16),
            pltpu.VMEM((SPAN * MP, 8, BLK), F32),
            pltpu.VMEM((BLK, DIM), F32),
            dma((slots,)),
            dma((slots,)),
            dma((SPAN * MP,)),
            dma((SPAN * MP,)),
            dma((slots,)),
            dma((slots,)),
            dma((2,)),
        ],
        compiler_params=pltpu.CompilerParams(
            collective_id=0, has_side_effects=True, vmem_limit_bytes=24 * 1024 * 1024
        ),
    )(
        queries.reshape(OWN, DIM),
        passages.transpose(1, 0, 2).reshape(ROWS, DIM),
        lengths,
        pos_index,
    )
    loss, qg, pg = pl.pallas_call(
        store,
        out_shape=tuple(jax.ShapeDtypeStruct(s, F32) for s in shapes),
        in_specs=[vmem] * 3,
        out_specs=(hbm,) * 3,
        scratch_shapes=[dma((3,))],
    )(*results)
    return (
        loss.reshape(PER),
        qg.reshape(PER, QTOK, DIM),
        pg.reshape(PTOK, PER, DIM).transpose(1, 0, 2),
    )


def solution(mesh):
    placed = (
        P(("blk", "mp"), None, None),
        P(("blk", "mp"), None, None),
        P(("blk", "mp")),
        P("blk", None),
    )
    return jax.shard_map(
        functools.partial(on_device, mesh.shape["blk"]),
        mesh=mesh,
        in_specs=placed,
        out_specs=(P(("blk", "mp")), P(("blk", "mp"), None, None), P(("blk", "mp"), None, None)),
        check_vma=False,
    )
```

```python
import functools
import math

import jax
import jax.numpy as jnp
from jax import lax
from jax.experimental import pallas as pl
from jax.experimental.pallas import tpu as pltpu
from jax.sharding import PartitionSpec as P

WINDOW = 4
SIDES = 2
CORES = 2
PER = 2
QTOK = 32
PTOK = 180
DIM = 128
ROWS = PER * PTOK
TILES = ROWS // 8
OWN = PER * QTOK
BLK = SIDES * OWN
RING_X = 4
LAYER = 32
NEG = -1e30
ROOT = DIM ** (-0.5)
MESH = pl.DeviceIdType.MESH
F32 = jnp.float32
BF16 = jnp.bfloat16


def spread_pairs(x):
    x = x + pltpu.roll(x, 4, 0)
    return x + pltpu.roll(x, 2, 0)


def max_pairs(x):
    x = jnp.maximum(x, pltpu.roll(x, 4, 0))
    return jnp.maximum(x, pltpu.roll(x, 2, 0))


def token_sum(x, same):
    hi = x.astype(BF16)
    rest = x - hi.astype(F32)
    mid = rest.astype(BF16)
    low = (rest - mid.astype(F32)).astype(BF16)
    dot = functools.partial(jnp.dot, preferred_element_type=F32)
    return dot(hi, same) + (dot(mid, same) + dot(low, same))


def work(
    blocks,
    q_hbm,
    p_hbm,
    len_hbm,
    pos_hbm,
    loss_ref,
    qg_ref,
    pg_ref,
    qall,
    p_ref,
    w_ref,
    msg_ref,
    sall,
    lens_ref,
    gsend,
    grecv,
    pgacc,
    pgrecv,
    lse_ref,
    len_ref,
    pos_ref,
    q_send,
    q_recv,
    s_send,
    s_recv,
    g_send,
    g_recv,
    pair_send,
    pair_recv,
    local,
):
    b = lax.axis_index("blk")
    m = lax.axis_index("mp")
    y = m // CORES
    core = m % CORES
    other = 1 - core

    def block(d):
        return lax.rem(b + (d + blocks), blocks)

    def remote(src, dst, send, recv, d, side, who):
        return pltpu.make_async_remote_copy(
            src_ref=src,
            dst_ref=dst,
            send_sem=send,
            recv_sem=recv,
            device_id={"blk": block(d), "mp": side * CORES + who},
            device_id_type=MESH,
        )

    def send_queries(s, k):
        side = (y + k) % SIDES
        return remote(
            q_hbm, qall.at[s, y], q_send.at[s * SIDES + k], q_recv.at[s * SIDES + y], s, side, core
        )

    def send_scores(s, t, k):
        side = (y + k) % SIDES
        return remote(
            msg_ref.at[s],
            sall.at[t, s * SIDES + y],
            s_send.at[(s * WINDOW + t) * SIDES + k],
            s_recv.at[(t * WINDOW + s) * SIDES + y],
            t - s,
            side,
            core,
        )

    def send_grads(s, k):
        side = (y + k) % SIDES
        return remote(
            gsend.at[s, side],
            grecv.at[s * SIDES + y],
            g_send.at[s * SIDES + k],
            g_recv.at[s * SIDES + y],
            -s,
            side,
            core,
        )

    barrier = pltpu.get_barrier_semaphore()
    near = [
        (d, k) for d in (3, 2, 1, -1, -2, -3, 0) for k in range(SIDES) if not (d == 0 and k == 0)
    ]
    for d, k in near:
        pl.semaphore_signal(
            barrier,
            inc=1,
            device_id={"blk": block(d), "mp": (y + k) % SIDES * CORES + core},
            device_id_type=MESH,
        )
    pl.semaphore_signal(
        barrier, inc=1, device_id={"blk": b, "mp": y * CORES + other}, device_id_type=MESH
    )
    get_len = pltpu.make_async_copy(len_hbm, len_ref, local.at[0])
    get_len.start()
    get_pos = pltpu.make_async_copy(pos_hbm, pos_ref, local.at[1])
    get_pos.start()
    get_q = pltpu.make_async_copy(q_hbm, qall.at[0, y], local.at[2])
    get_q.start()
    get_p = pltpu.make_async_copy(p_hbm, p_ref.at[core], local.at[3])
    get_p.start()
    pl.semaphore_wait(barrier, len(near) + 1)

    for s in (3, 2, 1, 0):
        for k in range(SIDES):
            if s or k:
                send_queries(s, k).start()
    pair_p = remote(p_hbm, p_ref.at[core], pair_send.at[0], pair_recv.at[0], 0, y, other)
    pair_p.start()

    row8 = lax.broadcasted_iota(jnp.int32, (8, BLK), 0)
    lane8 = lax.broadcasted_iota(jnp.int32, (8, BLK), 1)
    parity = row8 % 2
    half = row8 // 2 % 2
    get_len.wait()
    lens_ref[core] = jnp.where(parity == 0, len_ref[0], len_ref[1]).astype(F32)
    pair_len = remote(
        lens_ref.at[core], lens_ref.at[core], pair_send.at[1], pair_recv.at[1], 0, y, other
    )
    pair_len.start()
    get_pos.wait()
    query_of = lane8 // QTOK
    pos = jnp.zeros((8, BLK), jnp.int32)
    for side in range(SIDES):
        for i in range(PER):
            n = side * CORES * PER + core * PER + i
            pos = jnp.where(query_of == side * PER + i, pos_ref[0, n], pos)
    same = (
        lax.broadcasted_iota(jnp.int32, (BLK, BLK), 0) // QTOK
        == lax.broadcasted_iota(jnp.int32, (BLK, BLK), 1) // QTOK
    ).astype(F32).astype(BF16)
    token = (
        lax.broadcasted_iota(jnp.int32, (TILES, 8, BLK), 0) * 4
        + lax.broadcasted_iota(jnp.int32, (TILES, 8, BLK), 1) // 2
    )
    pgacc[...] = jnp.zeros_like(pgacc)
    get_p.wait()
    get_q.wait()
    pair_p.wait_recv()
    pair_len.wait_recv()

    def score_block(s, _):
        def arrived(side):
            remote(
                q_hbm, qall.at[s, side], q_send.at[0], q_recv.at[s * SIDES + side], 0, side, core
            ).wait_recv()

        arrived(1 - y)

        @pl.when(s > 0)
        def _():
            arrived(y)

        q_blk = qall[s].reshape(BLK, DIM)
        scores = []
        for h in range(CORES):
            logits = lax.dot_general(
                p_ref[h], q_blk, (((1,), (1,)), ((), ())), preferred_element_type=F32
            ).reshape(TILES, 8, BLK)
            lens = lens_ref[h]
            logits = jnp.where(token < lens.astype(jnp.int32)[None], logits, NEG)
            top = max_pairs(jnp.max(logits, axis=0))
            terms = jnp.exp2((logits - top[None]) * (ROOT * math.log2(math.e)))
            total = spread_pairs(jnp.sum(terms, axis=0))
            w_ref[s, h] = terms * (1.0 / total)[None]
            scores.append(token_sum(top * ROOT + jnp.log(total), same) - jnp.log(lens) * QTOK)
        message = jnp.where(half == 0, scores[0], scores[1])
        msg_ref[s] = message
        sall[s, s * SIDES + y] = message
        for u in range(WINDOW):
            t = (s + 1 + u) % WINDOW
            send_scores(s, t, 1).start()
            if u < WINDOW - 1:
                send_scores(s, t, 0).start()
        return 0

    def grad_block(s, _):
        for j in range(WINDOW):
            for side in range(SIDES):

                @pl.when((s != j) | (y != side))
                def _():
                    remote(
                        msg_ref.at[0],
                        sall.at[s, j * SIDES + side],
                        s_send.at[0],
                        s_recv.at[(s * WINDOW + j) * SIDES + side],
                        0,
                        side,
                        core,
                    ).wait_recv()

        tile = sall[s]
        top = jnp.max(tile, axis=0)
        top = jnp.maximum(top, pltpu.roll(top, 1, 0))
        top = jnp.maximum(top, pltpu.roll(top, 2, 0))
        total = jnp.sum(jnp.exp(tile - top[None]), axis=0)
        total = total + pltpu.roll(total, 1, 0)
        total = total + pltpu.roll(total, 2, 0)
        lse = top + jnp.log(total)
        lse_ref[s] = lse
        here = (pos == y * (CORES * PER) + row8 % (CORES * PER)) & (s == 0)
        coef = jnp.exp(msg_ref[s] - lse) - jnp.where(here, 1.0, 0.0)
        turned = pltpu.roll(coef, 2, 0)
        q_blk = qall[s].reshape(BLK, DIM)
        dq = jnp.zeros((BLK, DIM), F32)
        rows = []
        for h in range(CORES):
            c = jnp.where(half == h, coef, turned)
            d_rows = (w_ref[s, h] * c[None]).reshape(ROWS, BLK).astype(BF16)
            rows.append(d_rows)
            dq = dq + lax.dot_general(
                d_rows, p_ref[h], (((0,), (0,)), ((), ())), preferred_element_type=F32
            )
        gsend[s] = dq.astype(BF16).reshape(SIDES, OWN, DIM)
        send_grads(s, 1).start()

        @pl.when(s > 0)
        def _():
            send_grads(s, 0).start()

        for h in range(CORES):
            pgacc[h] += jnp.dot(rows[h], q_blk, preferred_element_type=F32)
        return 0

    early = jnp.where(b % LAYER < RING_X, b % RING_X + 1, WINDOW)

    def run(g, _):
        low = g * early
        high = early + g * (WINDOW - early)
        lax.fori_loop(low, high, score_block, 0)
        lax.fori_loop(low, high, grad_block, 0)
        return 0

    lax.fori_loop(0, 2, run, 0)

    pair_pg = remote(pgacc.at[other], pgrecv, pair_send.at[2], pair_recv.at[2], 0, y, other)
    pair_pg.start()

    found = jnp.zeros((8, BLK), F32)
    for side in range(SIDES):
        here = (pos == side * (CORES * PER) + row8) & (row8 < CORES * PER)
        found = found + jnp.where(here, sall[0, side], 0.0)
    loss = lse_ref[0][0:1] - jnp.sum(found, axis=0, keepdims=True)
    one = [
        jnp.sum(jnp.where(lane8[0:1] == y * OWN + n * QTOK, loss, 0.0)) for n in range(PER)
    ]
    place = lax.broadcasted_iota(jnp.int32, (1, PER), 1)
    loss_ref[...] = jnp.where(place == 0, one[0], one[1])

    qg = gsend[0, y].astype(F32)
    for s in range(WINDOW):
        for k in range(SIDES):
            if s or k:
                i = s * SIDES + (y + k) % SIDES
                remote(
                    gsend.at[0, 0], grecv.at[i], g_send.at[0], g_recv.at[i], 0, y, core
                ).wait_recv()
                qg = qg + grecv[i].astype(F32)
    qg_ref[...] = qg * ROOT
    pair_pg.wait_recv()
    pg_ref[...] = (pgacc[core] + pgrecv[...]) * ROOT

    pair_p.wait_send()
    pair_len.wait_send()
    pair_pg.wait_send()
    for s in range(WINDOW):
        for k in range(SIDES):
            if s or k:
                send_queries(s, k).wait_send()
                send_grads(s, k).wait_send()
            for t in range(WINDOW):
                if s != t or k:
                    send_scores(s, t, k).wait_send()


def store(loss_ref, qg_ref, pg_ref, loss_out, qg_out, pg_out, sems):
    copies = [
        pltpu.make_async_copy(src, dst, sems.at[i])
        for i, (src, dst) in enumerate(
            ((pg_ref, pg_out), (qg_ref, qg_out), (loss_ref, loss_out))
        )
    ]
    for c in copies:
        c.start()
    for c in copies:
        c.wait()


def on_device(blocks, queries, passages, lengths, pos_index):
    hbm = pl.BlockSpec(memory_space=pltpu.HBM)
    vmem = pl.BlockSpec(memory_space=pltpu.VMEM)
    shapes = ((1, PER), (OWN, DIM), (ROWS, DIM))
    slots = WINDOW * SIDES
    dma = pltpu.SemaphoreType.DMA
    operands = (
        queries.reshape(OWN, DIM),
        passages.transpose(1, 0, 2).reshape(ROWS, DIM),
        lengths,
        pos_index,
    )
    results = pl.pallas_call(
        functools.partial(work, blocks),
        out_shape=tuple(pltpu.VMEM(s, F32) for s in shapes),
        in_specs=[hbm] * 4,
        out_specs=(vmem,) * 3,
        scratch_shapes=[
            pltpu.VMEM((WINDOW, SIDES, OWN, DIM), BF16),
            pltpu.VMEM((CORES, ROWS, DIM), BF16),
            pltpu.VMEM((WINDOW, CORES, TILES, 8, BLK), F32),
            pltpu.VMEM((WINDOW, 8, BLK), F32),
            pltpu.VMEM((WINDOW, slots, 8, BLK), F32),
            pltpu.VMEM((CORES, 8, BLK), F32),
            pltpu.VMEM((WINDOW, SIDES, OWN, DIM), BF16),
            pltpu.VMEM((slots, OWN, DIM), BF16),
            pltpu.VMEM((CORES, ROWS, DIM), F32),
            pltpu.VMEM((ROWS, DIM), F32),
            pltpu.VMEM((WINDOW, 8, BLK), F32),
            pltpu.SMEM((PER,), jnp.int32),
            pltpu.SMEM((1, WINDOW * PER), jnp.int32),
            dma((slots,)),
            dma((slots,)),
            dma((WINDOW * slots,)),
            dma((WINDOW * slots,)),
            dma((slots,)),
            dma((slots,)),
            dma((3,)),
            dma((3,)),
            dma((4,)),
        ],
        compiler_params=pltpu.CompilerParams(
            collective_id=0, has_side_effects=True, vmem_limit_bytes=24 * 1024 * 1024
        ),
    )(*(pltpu.with_memory_space_constraint(x, pltpu.HBM) for x in operands))
    loss, qg, pg = pl.pallas_call(
        store,
        out_shape=tuple(pltpu.HBM(s, F32) for s in shapes),
        in_specs=[vmem] * 3,
        out_specs=(hbm,) * 3,
        scratch_shapes=[dma((3,))],
    )(*results)
    return (
        loss.reshape(PER),
        qg.reshape(PER, QTOK, DIM),
        pg.reshape(PTOK, PER, DIM).transpose(1, 0, 2),
    )


def solution(mesh):
    placed = (
        P(("blk", "mp"), None, None),
        P(("blk", "mp"), None, None),
        P(("blk", "mp")),
        P("blk", None),
    )
    return jax.shard_map(
        functools.partial(on_device, mesh.shape["blk"]),
        mesh=mesh,
        in_specs=placed,
        out_specs=(P(("blk", "mp")), P(("blk", "mp"), None, None), P(("blk", "mp"), None, None)),
        check_vma=False,
    )
```

```python
import functools
import math

import jax
import jax.numpy as jnp
from jax import lax
from jax.experimental import pallas as pl
from jax.experimental.pallas import tpu as pltpu
from jax.sharding import PartitionSpec as P

WINDOW = 4
SIDES = 2
CORES = 2
PER = 2
QTOK = 32
PTOK = 180
DIM = 128
ROWS = PER * PTOK
TILES = ROWS // 8
OWN = PER * QTOK
BLK = SIDES * OWN
RING_X = 4
LAYER = 32
NEG = -1e30
ROOT = DIM ** (-0.5)
MESH = pl.DeviceIdType.MESH
F32 = jnp.float32
BF16 = jnp.bfloat16


def spread_pairs(x):
    x = x + pltpu.roll(x, 4, 0)
    return x + pltpu.roll(x, 2, 0)


def max_pairs(x):
    x = jnp.maximum(x, pltpu.roll(x, 4, 0))
    return jnp.maximum(x, pltpu.roll(x, 2, 0))


def token_sum(x, same):
    hi = x.astype(BF16)
    rest = x - hi.astype(F32)
    mid = rest.astype(BF16)
    low = (rest - mid.astype(F32)).astype(BF16)
    dot = functools.partial(jnp.dot, preferred_element_type=F32)
    return dot(hi, same) + (dot(mid, same) + dot(low, same))


def work(
    blocks,
    q_hbm,
    p_hbm,
    len_hbm,
    pos_hbm,
    loss_ref,
    qg_ref,
    pg_ref,
    qall,
    p_ref,
    w_ref,
    msg_ref,
    sall,
    lens_ref,
    gsend,
    grecv,
    pgacc,
    pgrecv,
    d_ref,
    lse_ref,
    len_ref,
    pos_ref,
    q_send,
    q_recv,
    s_send,
    s_recv,
    g_send,
    g_recv,
    pair_send,
    pair_recv,
    local,
):
    b = lax.axis_index("blk")
    m = lax.axis_index("mp")
    y = m // CORES
    core = m % CORES
    other = 1 - core

    def block(d):
        return lax.rem(b + (d + blocks), blocks)

    def remote(src, dst, send, recv, d, side, who):
        return pltpu.make_async_remote_copy(
            src_ref=src,
            dst_ref=dst,
            send_sem=send,
            recv_sem=recv,
            device_id={"blk": block(d), "mp": side * CORES + who},
            device_id_type=MESH,
        )

    def send_queries(s, k):
        side = (y + k) % SIDES
        return remote(
            q_hbm, qall.at[s, y], q_send.at[s * SIDES + k], q_recv.at[s * SIDES + y], s, side, core
        )

    def send_scores(s, t, k):
        side = (y + k) % SIDES
        return remote(
            msg_ref.at[s],
            sall.at[t, s * SIDES + y],
            s_send.at[(s * WINDOW + t) * SIDES + k],
            s_recv.at[(t * WINDOW + s) * SIDES + y],
            t - s,
            side,
            core,
        )

    def send_grads(s, k):
        side = (y + k) % SIDES
        return remote(
            gsend.at[s, side],
            grecv.at[s * SIDES + y],
            g_send.at[s * SIDES + k],
            g_recv.at[s * SIDES + y],
            -s,
            side,
            core,
        )

    barrier = pltpu.get_barrier_semaphore()
    near = [(d, k) for d in (-3, -2, -1, 0) for k in range(SIDES) if d or k]
    for d, k in near:
        pl.semaphore_signal(
            barrier,
            inc=1,
            device_id={"blk": block(d), "mp": (y + k) % SIDES * CORES + core},
            device_id_type=MESH,
        )
    pl.semaphore_signal(
        barrier, inc=1, device_id={"blk": b, "mp": y * CORES + other}, device_id_type=MESH
    )
    get_len = pltpu.make_async_copy(len_hbm, len_ref, local.at[0])
    get_len.start()
    get_pos = pltpu.make_async_copy(pos_hbm, pos_ref, local.at[1])
    get_pos.start()
    get_q = pltpu.make_async_copy(q_hbm, qall.at[0, y], local.at[2])
    get_q.start()
    get_p = pltpu.make_async_copy(p_hbm, p_ref.at[core], local.at[3])
    get_p.start()
    pl.semaphore_wait(barrier, len(near) + 1)

    for s in (3, 2, 1, 0):
        for k in range(SIDES):
            if s or k:
                send_queries(s, k).start()
    pair_p = remote(p_hbm, p_ref.at[core], pair_send.at[0], pair_recv.at[0], 0, y, other)
    pair_p.start()

    row8 = lax.broadcasted_iota(jnp.int32, (8, BLK), 0)
    lane8 = lax.broadcasted_iota(jnp.int32, (8, BLK), 1)
    parity = row8 % 2
    half = row8 // 2 % 2
    get_len.wait()
    lens_ref[core] = jnp.where(parity == 0, len_ref[0], len_ref[1]).astype(F32)
    pair_len = remote(
        lens_ref.at[core], lens_ref.at[core], pair_send.at[1], pair_recv.at[1], 0, y, other
    )
    pair_len.start()
    get_pos.wait()
    query_of = lane8 // QTOK
    pos = jnp.zeros((8, BLK), jnp.int32)
    for side in range(SIDES):
        for i in range(PER):
            n = side * CORES * PER + core * PER + i
            pos = jnp.where(query_of == side * PER + i, pos_ref[0, n], pos)
    same = (
        lax.broadcasted_iota(jnp.int32, (BLK, BLK), 0) // QTOK
        == lax.broadcasted_iota(jnp.int32, (BLK, BLK), 1) // QTOK
    ).astype(F32).astype(BF16)
    token = (
        lax.broadcasted_iota(jnp.int32, (TILES, 8, BLK), 0) * 4
        + lax.broadcasted_iota(jnp.int32, (TILES, 8, BLK), 1) // 2
    )
    pgacc[...] = jnp.zeros_like(pgacc)
    get_p.wait()
    get_q.wait()
    pair_p.wait_recv()
    pair_len.wait_recv()

    def score_block(s, _):
        def arrived(side):
            remote(
                q_hbm, qall.at[s, side], q_send.at[0], q_recv.at[s * SIDES + side], 0, side, core
            ).wait_recv()

        arrived(1 - y)

        @pl.when(s > 0)
        def _():
            arrived(y)

        q_blk = qall[s].reshape(BLK, DIM)
        scores = []
        for h in range(CORES):
            logits = lax.dot_general(
                p_ref[h], q_blk, (((1,), (1,)), ((), ())), preferred_element_type=F32
            ).reshape(TILES, 8, BLK)
            lens = lens_ref[h]
            logits = jnp.where(token < lens.astype(jnp.int32)[None], logits, NEG)
            top = max_pairs(jnp.max(logits, axis=0))
            terms = jnp.exp2((logits - top[None]) * (ROOT * math.log2(math.e)))
            total = spread_pairs(jnp.sum(terms, axis=0))
            w_ref[s, h] = terms * (1.0 / total)[None]
            scores.append(token_sum(top * ROOT + jnp.log(total), same) - jnp.log(lens) * QTOK)
        message = jnp.where(half == 0, scores[0], scores[1])
        msg_ref[s] = message
        sall[s, s * SIDES + y] = message
        send_scores(s, s, 1).start()

        def ahead(t, _):
            for k in range(SIDES):
                send_scores(s, t, k).start()
            return 0

        lax.fori_loop(s + 1, WINDOW, ahead, 0)
        return 0

    def behind_block(s, _):
        def behind(t, _):
            for k in range(SIDES):
                send_scores(s, t, k).start()
            return 0

        lax.fori_loop(0, s, behind, 0)
        return 0

    def grad_block(s, _):
        for j in range(WINDOW):
            for side in range(SIDES):

                @pl.when((s != j) | (y != side))
                def _():
                    remote(
                        msg_ref.at[0],
                        sall.at[s, j * SIDES + side],
                        s_send.at[0],
                        s_recv.at[(s * WINDOW + j) * SIDES + side],
                        0,
                        side,
                        core,
                    ).wait_recv()

        tile = sall[s]
        top = jnp.max(tile, axis=0)
        top = jnp.maximum(top, pltpu.roll(top, 1, 0))
        top = jnp.maximum(top, pltpu.roll(top, 2, 0))
        total = jnp.sum(jnp.exp(tile - top[None]), axis=0)
        total = total + pltpu.roll(total, 1, 0)
        total = total + pltpu.roll(total, 2, 0)
        lse = top + jnp.log(total)
        lse_ref[s] = lse
        here = (pos == y * (CORES * PER) + row8 % (CORES * PER)) & (s == 0)
        coef = jnp.exp(msg_ref[s] - lse) - jnp.where(here, 1.0, 0.0)
        turned = pltpu.roll(coef, 2, 0)
        q_blk = qall[s].reshape(BLK, DIM)
        for h in range(CORES):
            c = jnp.where(half == h, coef, turned)
            d_rows = (w_ref[s, h] * c[None]).reshape(ROWS, BLK).astype(BF16)
            d_ref[s, h] = d_rows
            pgacc[h] += jnp.dot(d_rows, q_blk, preferred_element_type=F32)
        return 0

    def return_block(s, _):
        dq = jnp.zeros((BLK, DIM), F32)
        for h in range(CORES):
            dq = dq + lax.dot_general(
                d_ref[s, h], p_ref[h], (((0,), (0,)), ((), ())), preferred_element_type=F32
            )
        gsend[s] = dq.astype(BF16).reshape(SIDES, OWN, DIM)
        send_grads(s, 1).start()

        @pl.when(s > 0)
        def _():
            send_grads(s, 0).start()

        return 0

    early = jnp.where(b % LAYER < RING_X, b % RING_X + 1, WINDOW)

    def run(g, _):
        low = g * early
        high = early + g * (WINDOW - early)
        lax.fori_loop(low, high, score_block, 0)
        lax.fori_loop(low, high, behind_block, 0)
        lax.fori_loop(low, high, grad_block, 0)

        @pl.when(g == 1)
        def _():
            pair_pg.start()

        lax.fori_loop(low, high, return_block, 0)
        return 0

    pair_pg = remote(pgacc.at[other], pgrecv, pair_send.at[2], pair_recv.at[2], 0, y, other)
    lax.fori_loop(0, 2, run, 0)

    found = jnp.zeros((8, BLK), F32)
    for side in range(SIDES):
        here = (pos == side * (CORES * PER) + row8) & (row8 < CORES * PER)
        found = found + jnp.where(here, sall[0, side], 0.0)
    loss = lse_ref[0][0:1] - jnp.sum(found, axis=0, keepdims=True)
    one = [
        jnp.sum(jnp.where(lane8[0:1] == y * OWN + n * QTOK, loss, 0.0)) for n in range(PER)
    ]
    place = lax.broadcasted_iota(jnp.int32, (1, PER), 1)
    loss_ref[...] = jnp.where(place == 0, one[0], one[1])

    qg = gsend[0, y].astype(F32)
    for s in range(WINDOW):
        for k in range(SIDES):
            if s or k:
                i = s * SIDES + (y + k) % SIDES
                remote(
                    gsend.at[0, 0], grecv.at[i], g_send.at[0], g_recv.at[i], 0, y, core
                ).wait_recv()
                qg = qg + grecv[i].astype(F32)
    qg_ref[...] = qg * ROOT
    pair_pg.wait_recv()
    pg_ref[...] = (pgacc[core] + pgrecv[...]) * ROOT

    pair_p.wait_send()
    pair_len.wait_send()
    pair_pg.wait_send()
    for s in range(WINDOW):
        for k in range(SIDES):
            if s or k:
                send_queries(s, k).wait_send()
                send_grads(s, k).wait_send()
            for t in range(WINDOW):
                if s != t or k:
                    send_scores(s, t, k).wait_send()


def store(loss_ref, qg_ref, pg_ref, loss_out, qg_out, pg_out, sems):
    copies = [
        pltpu.make_async_copy(src, dst, sems.at[i])
        for i, (src, dst) in enumerate(
            ((pg_ref, pg_out), (qg_ref, qg_out), (loss_ref, loss_out))
        )
    ]
    for c in copies:
        c.start()
    for c in copies:
        c.wait()


def on_device(blocks, queries, passages, lengths, pos_index):
    hbm = pl.BlockSpec(memory_space=pltpu.HBM)
    vmem = pl.BlockSpec(memory_space=pltpu.VMEM)
    shapes = ((1, PER), (OWN, DIM), (ROWS, DIM))
    slots = WINDOW * SIDES
    dma = pltpu.SemaphoreType.DMA
    operands = (
        queries.reshape(OWN, DIM),
        passages.transpose(1, 0, 2).reshape(ROWS, DIM),
        lengths,
        pos_index,
    )
    results = pl.pallas_call(
        functools.partial(work, blocks),
        out_shape=tuple(pltpu.VMEM(s, F32) for s in shapes),
        in_specs=[hbm] * 4,
        out_specs=(vmem,) * 3,
        scratch_shapes=[
            pltpu.VMEM((WINDOW, SIDES, OWN, DIM), BF16),
            pltpu.VMEM((CORES, ROWS, DIM), BF16),
            pltpu.VMEM((WINDOW, CORES, TILES, 8, BLK), F32),
            pltpu.VMEM((WINDOW, 8, BLK), F32),
            pltpu.VMEM((WINDOW, slots, 8, BLK), F32),
            pltpu.VMEM((CORES, 8, BLK), F32),
            pltpu.VMEM((WINDOW, SIDES, OWN, DIM), BF16),
            pltpu.VMEM((slots, OWN, DIM), BF16),
            pltpu.VMEM((CORES, ROWS, DIM), F32),
            pltpu.VMEM((ROWS, DIM), F32),
            pltpu.VMEM((WINDOW, CORES, ROWS, BLK), BF16),
            pltpu.VMEM((WINDOW, 8, BLK), F32),
            pltpu.SMEM((PER,), jnp.int32),
            pltpu.SMEM((1, WINDOW * PER), jnp.int32),
            dma((slots,)),
            dma((slots,)),
            dma((WINDOW * slots,)),
            dma((WINDOW * slots,)),
            dma((slots,)),
            dma((slots,)),
            dma((3,)),
            dma((3,)),
            dma((4,)),
        ],
        compiler_params=pltpu.CompilerParams(
            collective_id=0, has_side_effects=True, vmem_limit_bytes=24 * 1024 * 1024
        ),
    )(*(pltpu.with_memory_space_constraint(x, pltpu.HBM) for x in operands))
    loss, qg, pg = pl.pallas_call(
        store,
        out_shape=tuple(pltpu.HBM(s, F32) for s in shapes),
        in_specs=[vmem] * 3,
        out_specs=(hbm,) * 3,
        scratch_shapes=[dma((3,))],
    )(*(pltpu.with_memory_space_constraint(x, pltpu.VMEM) for x in results))
    return (
        loss.reshape(PER),
        qg.reshape(PER, QTOK, DIM),
        pg.reshape(PTOK, PER, DIM).transpose(1, 0, 2),
    )


def solution(mesh):
    placed = (
        P(("blk", "mp"), None, None),
        P(("blk", "mp"), None, None),
        P(("blk", "mp")),
        P("blk", None),
    )
    return jax.shard_map(
        functools.partial(on_device, mesh.shape["blk"]),
        mesh=mesh,
        in_specs=placed,
        out_specs=(P(("blk", "mp")), P(("blk", "mp"), None, None), P(("blk", "mp"), None, None)),
        check_vma=False,
    )
```

```python
import functools
import math

import jax
import jax.numpy as jnp
from jax import lax
from jax.experimental import pallas as pl
from jax.experimental.pallas import tpu as pltpu
from jax.sharding import PartitionSpec as P

WINDOW = 4
SIDES = 2
CORES = 2
PER = 2
QTOK = 32
PTOK = 180
DIM = 128
ROWS = PER * PTOK
TILES = ROWS // 8
OWN = PER * QTOK
BLK = SIDES * OWN
RING_X = 4
LAYER = 32
NEG = -1e30
ROOT = DIM ** (-0.5)
MESH = pl.DeviceIdType.MESH
F32 = jnp.float32
BF16 = jnp.bfloat16


def spread_pairs(x):
    x = x + pltpu.roll(x, 4, 0)
    return x + pltpu.roll(x, 2, 0)


def max_pairs(x):
    x = jnp.maximum(x, pltpu.roll(x, 4, 0))
    return jnp.maximum(x, pltpu.roll(x, 2, 0))


def token_sum(x, same):
    hi = x.astype(BF16)
    rest = x - hi.astype(F32)
    mid = rest.astype(BF16)
    low = (rest - mid.astype(F32)).astype(BF16)
    pieces = jnp.concatenate([hi, mid, low], axis=1)
    return jnp.dot(pieces, same, preferred_element_type=F32)


def each(low, high, body):
    if isinstance(low, int) and isinstance(high, int):
        for i in range(low, high):
            body(i)
    else:
        lax.fori_loop(low, high, lambda i, _: body(i) or 0, 0)


def work(
    blocks,
    q_hbm,
    p_hbm,
    len_hbm,
    pos_hbm,
    loss_ref,
    qg_ref,
    pg_ref,
    qall,
    p_ref,
    w_ref,
    msg_ref,
    sall,
    lens_ref,
    left_ref,
    inverse_ref,
    gsend,
    grecv,
    pgacc,
    pgrecv,
    turned_p,
    lse_ref,
    len_ref,
    pos_ref,
    q_send,
    q_recv,
    s_send,
    s_recv,
    g_send,
    g_recv,
    pair_send,
    pair_recv,
    local,
):
    b = lax.axis_index("blk")
    m = lax.axis_index("mp")
    y = m // CORES
    core = m % CORES
    other = 1 - core

    def block(d):
        return lax.rem(b + (d + blocks), blocks)

    def remote(src, dst, send, recv, d, side, who):
        return pltpu.make_async_remote_copy(
            src_ref=src,
            dst_ref=dst,
            send_sem=send,
            recv_sem=recv,
            device_id={"blk": block(d), "mp": side * CORES + who},
            device_id_type=MESH,
        )

    def send_queries(s, k):
        side = (y + k) % SIDES
        return remote(
            q_hbm, qall.at[s, y], q_send.at[s * SIDES + k], q_recv.at[s * SIDES + y], s, side, core
        )

    def send_scores(s, t, k):
        side = (y + k) % SIDES
        return remote(
            msg_ref.at[s],
            sall.at[t, s * SIDES + y],
            s_send.at[(s * WINDOW + t) * SIDES + k],
            s_recv.at[(t * WINDOW + s) * SIDES + y],
            t - s,
            side,
            core,
        )

    def send_grads(s, k):
        side = (y + k) % SIDES
        return remote(
            gsend.at[s, side],
            grecv.at[s * SIDES + y],
            g_send.at[s * SIDES + k],
            g_recv.at[s * SIDES + y],
            -s,
            side,
            core,
        )

    barrier = pltpu.get_barrier_semaphore()
    near = [(d, k) for d in (0, -1, -2, -3) for k in range(SIDES) if d or k]
    pl.semaphore_signal(
        barrier, inc=1, device_id={"blk": b, "mp": y * CORES + other}, device_id_type=MESH
    )
    for d, k in near:
        pl.semaphore_signal(
            barrier,
            inc=1,
            device_id={"blk": block(d), "mp": (y + k) % SIDES * CORES + core},
            device_id_type=MESH,
        )
    pl.semaphore_wait(barrier, len(near) + 1)

    for i in range(WINDOW - 1):
        s = (WINDOW - 1 - b % RING_X + i) % (WINDOW - 1) + 1
        for k in range(SIDES):
            send_queries(s, k).start()
    send_queries(0, 1).start()
    get_len = pltpu.make_async_copy(len_hbm, len_ref, local.at[0])
    get_len.start()
    get_pos = pltpu.make_async_copy(pos_hbm, pos_ref, local.at[1])
    get_pos.start()
    get_q = pltpu.make_async_copy(q_hbm, qall.at[0, y], local.at[2])
    get_q.start()
    get_p = pltpu.make_async_copy(p_hbm, p_ref.at[core], local.at[3])
    get_p.start()
    pair_p = remote(p_hbm, p_ref.at[core], pair_send.at[0], pair_recv.at[0], 0, y, other)
    pair_p.start()

    row8 = lax.broadcasted_iota(jnp.int32, (8, BLK), 0)
    lane8 = lax.broadcasted_iota(jnp.int32, (8, BLK), 1)
    parity = row8 % 2
    half = row8 // 2 % 2
    get_len.wait()
    lens_ref[core] = jnp.where(parity == 0, len_ref[0], len_ref[1]).astype(F32)
    pair_len = remote(
        lens_ref.at[core], lens_ref.at[core], pair_send.at[1], pair_recv.at[1], 0, y, other
    )
    pair_len.start()
    get_pos.wait()
    query_of = lane8 // QTOK
    pos = jnp.zeros((8, BLK), jnp.int32)
    for side in range(SIDES):
        for i in range(PER):
            n = side * CORES * PER + core * PER + i
            pos = jnp.where(query_of == side * PER + i, pos_ref[0, n], pos)
    same = (
        lax.broadcasted_iota(jnp.int32, (BLK, BLK), 0) // QTOK
        == lax.broadcasted_iota(jnp.int32, (BLK, BLK), 1) // QTOK
    ).astype(F32).astype(BF16)
    same = jnp.concatenate([same] * 3, axis=0)
    first_token = lax.broadcasted_iota(jnp.int32, (TILES, 8, BLK), 0) * 4
    pgacc[...] = jnp.zeros_like(pgacc)
    get_p.wait()
    get_q.wait()
    pair_p.wait_recv()
    pair_len.wait_recv()
    log_len = jnp.log(jnp.where(half == 0, lens_ref[0], lens_ref[1])) * QTOK
    for h in range(CORES):
        left_ref[h] = lens_ref[h].astype(jnp.int32) - row8 // 2

    def score_block(s):
        def arrived(side):
            remote(
                q_hbm, qall.at[s, side], q_send.at[0], q_recv.at[s * SIDES + side], 0, side, core
            ).wait_recv()

        arrived(1 - y)

        @pl.when(s > 0)
        def _():
            arrived(y)

        q_blk = qall[s].reshape(BLK, DIM)
        tops = []
        totals = []
        for h in range(CORES):
            logits = lax.dot_general(
                p_ref[h], q_blk, (((1,), (1,)), ((), ())), preferred_element_type=F32
            ).reshape(TILES, 8, BLK)
            logits = jnp.where(left_ref[h][None] > first_token, logits, NEG)
            top = max_pairs(jnp.max(logits, axis=0))
            terms = jnp.exp2((logits - top[None]) * (ROOT * math.log2(math.e)))
            w_ref[s, h] = terms
            total = spread_pairs(jnp.sum(terms, axis=0))
            inverse_ref[s, h] = 1.0 / total
            tops.append(top)
            totals.append(total)
        top = jnp.where(half == 0, tops[0], tops[1])
        total = jnp.where(half == 0, totals[0], totals[1])
        message = token_sum(top * ROOT + jnp.log(total), same) - log_len
        msg_ref[s] = message
        sall[s, s * SIDES + y] = message
        send_scores(s, s, 1).start()

        def ahead(t):
            for k in range(SIDES):
                send_scores(s, t, k).start()

        each(s + 1, WINDOW, ahead)

    def behind_block(s):
        def behind(t):
            for k in range(SIDES):
                send_scores(s, t, k).start()

        each(0, s, behind)

    def grad_block(s):
        for j in range(WINDOW):
            for k in range(SIDES):
                side = (y + k) % SIDES

                @pl.when((s != j) | (k > 0))
                def _():
                    remote(
                        msg_ref.at[0],
                        sall.at[s, j * SIDES + side],
                        s_send.at[0],
                        s_recv.at[(s * WINDOW + j) * SIDES + side],
                        0,
                        side,
                        core,
                    ).wait_recv()

        tile = sall[s]
        top = jnp.max(tile, axis=0)
        top = jnp.maximum(top, pltpu.roll(top, 1, 0))
        top = jnp.maximum(top, pltpu.roll(top, 2, 0))
        total = jnp.sum(jnp.exp(tile - top[None]), axis=0)
        total = total + pltpu.roll(total, 1, 0)
        total = total + pltpu.roll(total, 2, 0)
        lse = top + jnp.log(total)
        lse_ref[s] = lse
        here = (pos == y * (CORES * PER) + row8 % (CORES * PER)) & (s == 0)
        coef = jnp.exp(msg_ref[s] - lse) - jnp.where(here, 1.0, 0.0)
        turned = pltpu.roll(coef, 2, 0)
        q_blk = qall[s].reshape(BLK, DIM)
        rows = []
        dq = jnp.zeros((DIM, BLK), F32)
        for h in range(CORES):
            c = jnp.where(half == h, coef, turned)
            c = c * inverse_ref[s, h]
            rows.append((w_ref[s, h] * c[None]).reshape(ROWS, BLK).astype(BF16))
            dq = dq + jnp.dot(turned_p[h], rows[h], preferred_element_type=F32)
        gsend[s] = dq.T.astype(BF16).reshape(SIDES, OWN, DIM)
        send_grads(s, 1).start()

        @pl.when(s > 0)
        def _():
            send_grads(s, 0).start()

        for h in range(CORES):
            pgacc[h] += jnp.dot(rows[h], q_blk, preferred_element_type=F32)

    def run(low, high):
        each(low, high, score_block)
        each(low, high, behind_block)
        each(0, high - low, lambda i: grad_block(high - 1 - i))

    place_x = b % RING_X
    first_layer = b % LAYER < RING_X
    early = jnp.where(first_layer, place_x + 1, WINDOW)
    each(0, early, score_block)
    each(0, early, behind_block)
    for h in range(CORES):
        turned_p[h] = p_ref[h].astype(F32).T.astype(BF16)
    each(0, early, lambda i: grad_block(early - 1 - i))
    for x in range(WINDOW - 1):
        pl.when(first_layer & (place_x == x))(functools.partial(run, x + 1, WINDOW))

    pair_pg = remote(pgacc.at[other], pgrecv, pair_send.at[2], pair_recv.at[2], 0, y, other)
    pair_pg.start()

    found = jnp.zeros((8, BLK), F32)
    for side in range(SIDES):
        here = (pos == side * (CORES * PER) + row8) & (row8 < CORES * PER)
        found = found + jnp.where(here, sall[0, side], 0.0)
    loss = lse_ref[0][0:1] - jnp.sum(found, axis=0, keepdims=True)
    one = [
        jnp.sum(jnp.where(lane8[0:1] == y * OWN + n * QTOK, loss, 0.0)) for n in range(PER)
    ]
    place = lax.broadcasted_iota(jnp.int32, (1, PER), 1)
    loss_ref[...] = jnp.where(place == 0, one[0], one[1])

    qg = gsend[0, y].astype(F32)
    for s in range(WINDOW):
        for k in range(SIDES):
            if s or k:
                i = s * SIDES + (y + k) % SIDES
                remote(
                    gsend.at[0, 0], grecv.at[i], g_send.at[0], g_recv.at[i], 0, y, core
                ).wait_recv()
                qg = qg + grecv[i].astype(F32)
    qg_ref[...] = qg * ROOT
    pair_pg.wait_recv()
    pg_ref[...] = (pgacc[core] + pgrecv[...]) * ROOT

    pair_p.wait_send()
    pair_len.wait_send()
    pair_pg.wait_send()
    for s in range(WINDOW):
        for k in range(SIDES):
            if s or k:
                send_queries(s, k).wait_send()
                send_grads(s, k).wait_send()
            for t in range(WINDOW):
                if s != t or k:
                    send_scores(s, t, k).wait_send()


def store(loss_ref, qg_ref, pg_ref, loss_out, qg_out, pg_out, sems):
    copies = [
        pltpu.make_async_copy(src, dst, sems.at[i])
        for i, (src, dst) in enumerate(
            ((pg_ref, pg_out), (qg_ref, qg_out), (loss_ref, loss_out))
        )
    ]
    for c in copies:
        c.start()
    for c in copies:
        c.wait()


def on_device(blocks, queries, passages, lengths, pos_index):
    hbm = pl.BlockSpec(memory_space=pltpu.HBM)
    vmem = pl.BlockSpec(memory_space=pltpu.VMEM)
    shapes = ((1, PER), (OWN, DIM), (ROWS, DIM))
    slots = WINDOW * SIDES
    dma = pltpu.SemaphoreType.DMA
    operands = (
        queries.reshape(OWN, DIM),
        passages.transpose(1, 0, 2).reshape(ROWS, DIM),
        lengths,
        pos_index,
    )
    results = pl.pallas_call(
        functools.partial(work, blocks),
        out_shape=tuple(pltpu.VMEM(s, F32) for s in shapes),
        in_specs=[hbm] * 4,
        out_specs=(vmem,) * 3,
        scratch_shapes=[
            pltpu.VMEM((WINDOW, SIDES, OWN, DIM), BF16),
            pltpu.VMEM((CORES, ROWS, DIM), BF16),
            pltpu.VMEM((WINDOW, CORES, TILES, 8, BLK), F32),
            pltpu.VMEM((WINDOW, 8, BLK), F32),
            pltpu.VMEM((WINDOW, slots, 8, BLK), F32),
            pltpu.VMEM((CORES, 8, BLK), F32),
            pltpu.VMEM((CORES, 8, BLK), jnp.int32),
            pltpu.VMEM((WINDOW, CORES, 8, BLK), F32),
            pltpu.VMEM((WINDOW, SIDES, OWN, DIM), BF16),
            pltpu.VMEM((slots, OWN, DIM), BF16),
            pltpu.VMEM((CORES, ROWS, DIM), F32),
            pltpu.VMEM((ROWS, DIM), F32),
            pltpu.VMEM((CORES, DIM, ROWS), BF16),
            pltpu.VMEM((WINDOW, 8, BLK), F32),
            pltpu.SMEM((PER,), jnp.int32),
            pltpu.SMEM((1, WINDOW * PER), jnp.int32),
            dma((slots,)),
            dma((slots,)),
            dma((WINDOW * slots,)),
            dma((WINDOW * slots,)),
            dma((slots,)),
            dma((slots,)),
            dma((3,)),
            dma((3,)),
            dma((4,)),
        ],
        compiler_params=pltpu.CompilerParams(
            collective_id=0, has_side_effects=True, vmem_limit_bytes=24 * 1024 * 1024
        ),
    )(*(pltpu.with_memory_space_constraint(x, pltpu.HBM) for x in operands))
    loss, qg, pg = pl.pallas_call(
        store,
        out_shape=tuple(pltpu.HBM(s, F32) for s in shapes),
        in_specs=[vmem] * 3,
        out_specs=(hbm,) * 3,
        scratch_shapes=[dma((3,))],
    )(*(pltpu.with_memory_space_constraint(x, pltpu.VMEM) for x in results))
    return (
        loss.reshape(PER),
        qg.reshape(PER, QTOK, DIM),
        pg.reshape(PTOK, PER, DIM).transpose(1, 0, 2),
    )


def solution(mesh):
    placed = (
        P(("blk", "mp"), None, None),
        P(("blk", "mp"), None, None),
        P(("blk", "mp")),
        P("blk", None),
    )
    return jax.shard_map(
        functools.partial(on_device, mesh.shape["blk"]),
        mesh=mesh,
        in_specs=placed,
        out_specs=(P(("blk", "mp")), P(("blk", "mp"), None, None), P(("blk", "mp"), None, None)),
        check_vma=False,
    )
```

```python
import functools
import math

import jax
import jax.numpy as jnp
from jax import lax
from jax.experimental import pallas as pl
from jax.experimental.pallas import tpu as pltpu
from jax.sharding import PartitionSpec as P

WINDOW = 4
SIDES = 2
CORES = 2
PER = 2
CANDS = CORES * PER
QTOK = 32
PTOK = 180
DIM = 128
ROWS = PER * PTOK
TILES = ROWS // 8
OWN = PER * QTOK
BLK = SIDES * OWN
RING_X = 4
LAYER = 32
NEG = -1e30
ROOT = DIM ** (-0.5)
MESH = pl.DeviceIdType.MESH
F32 = jnp.float32
BF16 = jnp.bfloat16


def spread_pairs(x):
    x = x + pltpu.roll(x, 4, 0)
    return x + pltpu.roll(x, 2, 0)


def max_pairs(x):
    x = jnp.maximum(x, pltpu.roll(x, 4, 0))
    return jnp.maximum(x, pltpu.roll(x, 2, 0))


def token_sum(x, same):
    hi = x.astype(BF16)
    rest = x - hi.astype(F32)
    mid = rest.astype(BF16)
    low = (rest - mid.astype(F32)).astype(BF16)
    pieces = jnp.concatenate([hi, mid, low], axis=1)
    return jnp.dot(pieces, same, preferred_element_type=F32)


def each(low, high, body):
    if isinstance(low, int) and isinstance(high, int):
        for i in range(low, high):
            body(i)
    else:
        lax.fori_loop(low, high, lambda i, _: body(i) or 0, 0)


def work(
    blocks,
    q_hbm,
    p_hbm,
    len_hbm,
    pos_hbm,
    loss_ref,
    qg_ref,
    pg_ref,
    qall,
    p_ref,
    w_ref,
    own_ref,
    msg_ref,
    sall,
    lens_ref,
    left_ref,
    inverse_ref,
    gsend,
    grecv,
    pgacc,
    pgrecv,
    turned_p,
    lse_ref,
    len_ref,
    pos_ref,
    q_send,
    q_recv,
    s_send,
    s_recv,
    g_send,
    g_recv,
    pair_send,
    pair_recv,
    local,
):
    b = lax.axis_index("blk")
    m = lax.axis_index("mp")
    y = m // CORES
    core = m % CORES
    other = 1 - core

    def block(d):
        return lax.rem(b + (d + blocks), blocks)

    def remote(src, dst, send, recv, d, side, who):
        return pltpu.make_async_remote_copy(
            src_ref=src,
            dst_ref=dst,
            send_sem=send,
            recv_sem=recv,
            device_id={"blk": block(d), "mp": side * CORES + who},
            device_id_type=MESH,
        )

    def send_queries(s, k):
        side = (y + k) % SIDES
        return remote(
            q_hbm, qall.at[s, y], q_send.at[s * SIDES + k], q_recv.at[s * SIDES + y], s, side, core
        )

    def send_scores(s, t, k):
        side = (y + k) % SIDES
        return remote(
            msg_ref.at[s],
            sall.at[t, s, y],
            s_send.at[(s * WINDOW + t) * SIDES + k],
            s_recv.at[(t * WINDOW + s) * SIDES + y],
            t - s,
            side,
            core,
        )

    def send_grads(s, k):
        side = (y + k) % SIDES
        return remote(
            gsend.at[s, side],
            grecv.at[s * SIDES + y],
            g_send.at[s * SIDES + k],
            g_recv.at[s * SIDES + y],
            -s,
            side,
            core,
        )

    barrier = pltpu.get_barrier_semaphore()
    near = [(d, k) for d in (0, -1, -2, -3) for k in range(SIDES) if d or k]
    pl.semaphore_signal(
        barrier, inc=1, device_id={"blk": b, "mp": y * CORES + other}, device_id_type=MESH
    )
    for d, k in near:
        pl.semaphore_signal(
            barrier,
            inc=1,
            device_id={"blk": block(d), "mp": (y + k) % SIDES * CORES + core},
            device_id_type=MESH,
        )
    pl.semaphore_wait(barrier, len(near) + 1)

    for i in range(WINDOW - 1):
        s = (WINDOW - 1 - b % RING_X + i) % (WINDOW - 1) + 1
        for k in range(SIDES):
            send_queries(s, k).start()
    send_queries(0, 1).start()
    get_len = pltpu.make_async_copy(len_hbm, len_ref, local.at[0])
    get_len.start()
    get_pos = pltpu.make_async_copy(pos_hbm, pos_ref, local.at[1])
    get_pos.start()
    get_q = pltpu.make_async_copy(q_hbm, qall.at[0, y], local.at[2])
    get_q.start()
    get_p = pltpu.make_async_copy(p_hbm, p_ref.at[core], local.at[3])
    get_p.start()
    pair_p = remote(p_hbm, p_ref.at[core], pair_send.at[0], pair_recv.at[0], 0, y, other)
    pair_p.start()

    row8 = lax.broadcasted_iota(jnp.int32, (8, BLK), 0)
    lane8 = lax.broadcasted_iota(jnp.int32, (8, BLK), 1)
    parity = row8 % 2
    half = row8 // 2 % 2
    get_len.wait()
    lens_ref[core] = jnp.where(parity == 0, len_ref[0], len_ref[1]).astype(F32)
    pair_len = remote(
        lens_ref.at[core], lens_ref.at[core], pair_send.at[1], pair_recv.at[1], 0, y, other
    )
    pair_len.start()
    get_pos.wait()
    query_of = lane8 // QTOK
    pos = jnp.zeros((8, BLK), jnp.int32)
    for side in range(SIDES):
        for i in range(PER):
            n = side * CORES * PER + core * PER + i
            pos = jnp.where(query_of == side * PER + i, pos_ref[0, n], pos)
    same = (
        lax.broadcasted_iota(jnp.int32, (BLK, BLK), 0) // QTOK
        == lax.broadcasted_iota(jnp.int32, (BLK, BLK), 1) // QTOK
    ).astype(F32).astype(BF16)
    same = jnp.concatenate([same] * 3, axis=0)
    first_token = lax.broadcasted_iota(jnp.int32, (TILES, 8, BLK), 0) * 4
    pgacc[...] = jnp.zeros_like(pgacc)
    get_p.wait()
    get_q.wait()
    pair_p.wait_recv()
    pair_len.wait_recv()
    log_len = jnp.log(jnp.where(half == 0, lens_ref[0], lens_ref[1])) * QTOK
    for h in range(CORES):
        left_ref[h] = lens_ref[h].astype(jnp.int32) - row8 // 2

    def score_block(s):
        def arrived(side):
            remote(
                q_hbm, qall.at[s, side], q_send.at[0], q_recv.at[s * SIDES + side], 0, side, core
            ).wait_recv()

        arrived(1 - y)

        @pl.when(s > 0)
        def _():
            arrived(y)

        q_blk = qall[s].reshape(BLK, DIM)
        tops = []
        totals = []
        for h in range(CORES):
            logits = lax.dot_general(
                p_ref[h], q_blk, (((1,), (1,)), ((), ())), preferred_element_type=F32
            ).reshape(TILES, 8, BLK)
            logits = jnp.where(left_ref[h][None] > first_token, logits, NEG)
            top = max_pairs(jnp.max(logits, axis=0))
            terms = jnp.exp2((logits - top[None]) * (ROOT * math.log2(math.e)))
            w_ref[s, h] = terms
            total = spread_pairs(jnp.sum(terms, axis=0))
            inverse_ref[s, h] = 1.0 / total
            tops.append(top)
            totals.append(total)
        top = jnp.where(half == 0, tops[0], tops[1])
        total = jnp.where(half == 0, totals[0], totals[1])
        message = token_sum(top * ROOT + jnp.log(total), same) - log_len
        own_ref[s] = message
        msg_ref[s] = message[:CANDS]
        sall[s, s, y] = message[:CANDS]
        send_scores(s, s, 1).start()

        def ahead(t):
            for k in range(SIDES):
                send_scores(s, t, k).start()

        each(s + 1, WINDOW, ahead)

    def behind_block(s):
        def behind(t):
            for k in range(SIDES):
                send_scores(s, t, k).start()

        each(0, s, behind)

    def grad_block(s):
        for j in range(WINDOW):
            for k in range(SIDES):
                side = (y + k) % SIDES

                @pl.when((s != j) | (k > 0))
                def _():
                    remote(
                        msg_ref.at[0],
                        sall.at[s, j, side],
                        s_send.at[0],
                        s_recv.at[(s * WINDOW + j) * SIDES + side],
                        0,
                        side,
                        core,
                    ).wait_recv()

        tile = sall[s]
        top = jnp.max(jnp.max(tile, axis=(0, 1)), axis=0, keepdims=True)
        terms = jnp.sum(jnp.exp(tile - top[None, None]), axis=(0, 1))
        lse = top + jnp.log(jnp.sum(terms, axis=0, keepdims=True))
        lse = jnp.broadcast_to(lse, (8, BLK))
        lse_ref[s] = lse
        here = (pos == y * (CORES * PER) + row8 % (CORES * PER)) & (s == 0)
        coef = jnp.exp(own_ref[s] - lse) - jnp.where(here, 1.0, 0.0)
        turned = pltpu.roll(coef, 2, 0)
        q_blk = qall[s].reshape(BLK, DIM)
        rows = []
        dq = jnp.zeros((DIM, BLK), F32)
        for h in range(CORES):
            c = jnp.where(half == h, coef, turned)
            c = c * inverse_ref[s, h]
            rows.append((w_ref[s, h] * c[None]).reshape(ROWS, BLK).astype(BF16))
            dq = dq + jnp.dot(turned_p[h], rows[h], preferred_element_type=F32)
        gsend[s] = dq.T.astype(BF16).reshape(SIDES, OWN, DIM)
        send_grads(s, 1).start()

        @pl.when(s > 0)
        def _():
            send_grads(s, 0).start()

        for h in range(CORES):
            pgacc[h] += jnp.dot(rows[h], q_blk, preferred_element_type=F32)

    def run(low, high):
        each(low, high, score_block)
        each(low, high, behind_block)
        each(0, high - low, lambda i: grad_block(high - 1 - i))

    place_x = b % RING_X
    first_layer = b % LAYER < RING_X
    early = jnp.where(first_layer, place_x + 1, WINDOW)
    each(0, early, score_block)
    each(0, early, behind_block)
    for h in range(CORES):
        turned_p[h] = p_ref[h].astype(F32).T.astype(BF16)
    each(0, early, lambda i: grad_block(early - 1 - i))
    for x in range(WINDOW - 1):
        pl.when(first_layer & (place_x == x))(functools.partial(run, x + 1, WINDOW))

    pair_pg = remote(pgacc.at[other], pgrecv, pair_send.at[2], pair_recv.at[2], 0, y, other)
    pair_pg.start()

    found = jnp.zeros((CANDS, BLK), F32)
    for side in range(SIDES):
        here = pos[:CANDS] == side * CANDS + row8[:CANDS]
        found = found + jnp.where(here, sall[0, 0, side], 0.0)
    loss = lse_ref[0][0:1] - jnp.sum(found, axis=0, keepdims=True)
    one = [
        jnp.sum(jnp.where(lane8[0:1] == y * OWN + n * QTOK, loss, 0.0)) for n in range(PER)
    ]
    place = lax.broadcasted_iota(jnp.int32, (1, PER), 1)
    loss_ref[...] = jnp.where(place == 0, one[0], one[1])

    qg = gsend[0, y].astype(F32)
    for s in range(WINDOW):
        for k in range(SIDES):
            if s or k:
                i = s * SIDES + (y + k) % SIDES
                remote(
                    gsend.at[0, 0], grecv.at[i], g_send.at[0], g_recv.at[i], 0, y, core
                ).wait_recv()
                qg = qg + grecv[i].astype(F32)
    qg_ref[...] = qg * ROOT
    pair_pg.wait_recv()
    pg_ref[...] = (pgacc[core] + pgrecv[...]) * ROOT

    pair_p.wait_send()
    pair_len.wait_send()
    pair_pg.wait_send()
    for s in range(WINDOW):
        for k in range(SIDES):
            if s or k:
                send_queries(s, k).wait_send()
                send_grads(s, k).wait_send()
            for t in range(WINDOW):
                if s != t or k:
                    send_scores(s, t, k).wait_send()


def store(loss_ref, qg_ref, pg_ref, loss_out, qg_out, pg_out, sems):
    copies = [
        pltpu.make_async_copy(src, dst, sems.at[i])
        for i, (src, dst) in enumerate(
            ((pg_ref, pg_out), (qg_ref, qg_out), (loss_ref, loss_out))
        )
    ]
    for c in copies:
        c.start()
    for c in copies:
        c.wait()


def on_device(blocks, queries, passages, lengths, pos_index):
    hbm = pl.BlockSpec(memory_space=pltpu.HBM)
    vmem = pl.BlockSpec(memory_space=pltpu.VMEM)
    shapes = ((1, PER), (OWN, DIM), (ROWS, DIM))
    slots = WINDOW * SIDES
    dma = pltpu.SemaphoreType.DMA
    operands = (
        queries.reshape(OWN, DIM),
        passages.transpose(1, 0, 2).reshape(ROWS, DIM),
        lengths,
        pos_index,
    )
    results = pl.pallas_call(
        functools.partial(work, blocks),
        out_shape=tuple(pltpu.VMEM(s, F32) for s in shapes),
        in_specs=[hbm] * 4,
        out_specs=(vmem,) * 3,
        scratch_shapes=[
            pltpu.VMEM((WINDOW, SIDES, OWN, DIM), BF16),
            pltpu.VMEM((CORES, ROWS, DIM), BF16),
            pltpu.VMEM((WINDOW, CORES, TILES, 8, BLK), F32),
            pltpu.VMEM((WINDOW, 8, BLK), F32),
            pltpu.VMEM((WINDOW, CANDS, BLK), F32),
            pltpu.VMEM((WINDOW, WINDOW, SIDES, CANDS, BLK), F32),
            pltpu.VMEM((CORES, 8, BLK), F32),
            pltpu.VMEM((CORES, 8, BLK), jnp.int32),
            pltpu.VMEM((WINDOW, CORES, 8, BLK), F32),
            pltpu.VMEM((WINDOW, SIDES, OWN, DIM), BF16),
            pltpu.VMEM((slots, OWN, DIM), BF16),
            pltpu.VMEM((CORES, ROWS, DIM), F32),
            pltpu.VMEM((ROWS, DIM), F32),
            pltpu.VMEM((CORES, DIM, ROWS), BF16),
            pltpu.VMEM((WINDOW, 8, BLK), F32),
            pltpu.SMEM((PER,), jnp.int32),
            pltpu.SMEM((1, WINDOW * PER), jnp.int32),
            dma((slots,)),
            dma((slots,)),
            dma((WINDOW * slots,)),
            dma((WINDOW * slots,)),
            dma((slots,)),
            dma((slots,)),
            dma((3,)),
            dma((3,)),
            dma((4,)),
        ],
        compiler_params=pltpu.CompilerParams(
            collective_id=0, has_side_effects=True, vmem_limit_bytes=24 * 1024 * 1024
        ),
    )(*(pltpu.with_memory_space_constraint(x, pltpu.HBM) for x in operands))
    loss, qg, pg = pl.pallas_call(
        store,
        out_shape=tuple(pltpu.HBM(s, F32) for s in shapes),
        in_specs=[vmem] * 3,
        out_specs=(hbm,) * 3,
        scratch_shapes=[dma((3,))],
    )(*(pltpu.with_memory_space_constraint(x, pltpu.VMEM) for x in results))
    return (
        loss.reshape(PER),
        qg.reshape(PER, QTOK, DIM),
        pg.reshape(PTOK, PER, DIM).transpose(1, 0, 2),
    )


def solution(mesh):
    placed = (
        P(("blk", "mp"), None, None),
        P(("blk", "mp"), None, None),
        P(("blk", "mp")),
        P("blk", None),
    )
    return jax.shard_map(
        functools.partial(on_device, mesh.shape["blk"]),
        mesh=mesh,
        in_specs=placed,
        out_specs=(P(("blk", "mp")), P(("blk", "mp"), None, None), P(("blk", "mp"), None, None)),
        check_vma=False,
    )
```

```python
import functools
import math

import jax
import jax.numpy as jnp
from jax import lax
from jax.experimental import pallas as pl
from jax.experimental.pallas import tpu as pltpu
from jax.sharding import PartitionSpec as P

WINDOW = 4
SIDES = 2
CORES = 2
PER = 2
CANDS = CORES * PER
QTOK = 32
PTOK = 180
DIM = 128
ROWS = PER * PTOK
TILES = ROWS // 8
OWN = PER * QTOK
BLK = SIDES * OWN
RING_X = 4
LAYER = 32
NEG = -1e30
ROOT = DIM ** (-0.5)
MESH = pl.DeviceIdType.MESH
F32 = jnp.float32
BF16 = jnp.bfloat16


def spread_pairs(x):
    x = x + pltpu.roll(x, 4, 0)
    return x + pltpu.roll(x, 2, 0)


def max_pairs(x):
    x = jnp.maximum(x, pltpu.roll(x, 4, 0))
    return jnp.maximum(x, pltpu.roll(x, 2, 0))


def token_sum(x, same):
    hi = x.astype(BF16)
    rest = x - hi.astype(F32)
    mid = rest.astype(BF16)
    low = (rest - mid.astype(F32)).astype(BF16)
    pieces = jnp.concatenate([hi, mid, low], axis=1)
    return jnp.dot(pieces, same, preferred_element_type=F32)


def each(low, high, body):
    if isinstance(low, int) and isinstance(high, int):
        for i in range(low, high):
            body(i)
    else:
        lax.fori_loop(low, high, lambda i, _: body(i) or 0, 0)


def work(
    blocks,
    q_hbm,
    p_hbm,
    len_hbm,
    pos_hbm,
    loss_ref,
    qg_ref,
    pg_ref,
    qall,
    p_ref,
    w_ref,
    own_ref,
    msg_ref,
    sall,
    lens_ref,
    left_ref,
    inverse_ref,
    gsend,
    grecv,
    pgacc,
    pgrecv,
    turned_p,
    lse_ref,
    len_ref,
    pos_ref,
    q_send,
    q_recv,
    s_send,
    s_recv,
    g_send,
    g_recv,
    pair_send,
    pair_recv,
    local,
):
    b = lax.axis_index("blk")
    m = lax.axis_index("mp")
    y = m // CORES
    core = m % CORES
    other = 1 - core

    def block(d):
        return lax.rem(b + (d + blocks), blocks)

    def remote(src, dst, send, recv, d, side, who):
        return pltpu.make_async_remote_copy(
            src_ref=src,
            dst_ref=dst,
            send_sem=send,
            recv_sem=recv,
            device_id={"blk": block(d), "mp": side * CORES + who},
            device_id_type=MESH,
        )

    def send_queries(s, k):
        side = (y + k) % SIDES
        return remote(
            qall.at[0, y], qall.at[s, y], q_send.at[s * SIDES + k], q_recv.at[s * SIDES + y], s, side, core
        )

    def send_scores(s, t, k):
        side = (y + k) % SIDES
        return remote(
            msg_ref.at[s],
            sall.at[t, s, y],
            s_send.at[(s * WINDOW + t) * SIDES + k],
            s_recv.at[(t * WINDOW + s) * SIDES + y],
            t - s,
            side,
            core,
        )

    def send_grads(s, k):
        side = (y + k) % SIDES
        return remote(
            gsend.at[s, side],
            grecv.at[s * SIDES + y],
            g_send.at[s * SIDES + k],
            g_recv.at[s * SIDES + y],
            -s,
            side,
            core,
        )

    barrier = pltpu.get_barrier_semaphore()
    pl.semaphore_signal(
        barrier, inc=1, device_id={"blk": b, "mp": y * CORES + other}, device_id_type=MESH
    )
    get_len = pltpu.make_async_copy(len_hbm, len_ref, local.at[0])
    get_len.start()
    get_pos = pltpu.make_async_copy(pos_hbm, pos_ref, local.at[1])
    get_pos.start()
    get_q = pltpu.make_async_copy(q_hbm, qall.at[0, y], local.at[2])
    get_q.start()
    get_p = pltpu.make_async_copy(p_hbm, p_ref.at[core], local.at[3])
    get_p.start()

    near = [(d, k) for d in (0, -1, -2, -3) for k in range(SIDES) if d or k]
    for d, k in near:
        pl.semaphore_signal(
            barrier,
            inc=1,
            device_id={"blk": block(d), "mp": (y + k) % SIDES * CORES + core},
            device_id_type=MESH,
        )
    get_q.wait()
    pl.semaphore_wait(barrier, len(near) + 1)

    for i in range(WINDOW - 1):
        s = (WINDOW - 1 - b % RING_X + i) % (WINDOW - 1) + 1
        for k in range(SIDES):
            send_queries(s, k).start()
    send_queries(0, 1).start()
    get_p.wait()
    pair_p = remote(p_ref.at[core], p_ref.at[core], pair_send.at[0], pair_recv.at[0], 0, y, other)
    pair_p.start()

    row8 = lax.broadcasted_iota(jnp.int32, (8, BLK), 0)
    lane8 = lax.broadcasted_iota(jnp.int32, (8, BLK), 1)
    parity = row8 % 2
    half = row8 // 2 % 2
    get_len.wait()
    lens_ref[core] = jnp.where(parity == 0, len_ref[0], len_ref[1]).astype(F32)
    pair_len = remote(
        lens_ref.at[core], lens_ref.at[core], pair_send.at[1], pair_recv.at[1], 0, y, other
    )
    pair_len.start()
    get_pos.wait()
    query_of = lane8 // QTOK
    pos = jnp.zeros((8, BLK), jnp.int32)
    for side in range(SIDES):
        for i in range(PER):
            n = side * CORES * PER + core * PER + i
            pos = jnp.where(query_of == side * PER + i, pos_ref[0, n], pos)
    same = (
        lax.broadcasted_iota(jnp.int32, (BLK, BLK), 0) // QTOK
        == lax.broadcasted_iota(jnp.int32, (BLK, BLK), 1) // QTOK
    ).astype(F32).astype(BF16)
    same = jnp.concatenate([same] * 3, axis=0)
    first_token = lax.broadcasted_iota(jnp.int32, (TILES, 8, BLK), 0) * 4
    pgacc[...] = jnp.zeros_like(pgacc)
    pair_p.wait_recv()
    pair_len.wait_recv()
    log_len = jnp.log(jnp.where(half == 0, lens_ref[0], lens_ref[1])) * QTOK
    for h in range(CORES):
        left_ref[h] = lens_ref[h].astype(jnp.int32) - row8 // 2

    def score_block(s):
        def arrived(side):
            remote(
                q_hbm, qall.at[s, side], q_send.at[0], q_recv.at[s * SIDES + side], 0, side, core
            ).wait_recv()

        arrived(1 - y)

        @pl.when(s > 0)
        def _():
            arrived(y)

        q_blk = qall[s].reshape(BLK, DIM)
        tops = []
        totals = []
        for h in range(CORES):
            logits = lax.dot_general(
                p_ref[h], q_blk, (((1,), (1,)), ((), ())), preferred_element_type=F32
            ).reshape(TILES, 8, BLK)
            logits = jnp.where(left_ref[h][None] > first_token, logits, NEG)
            top = max_pairs(jnp.max(logits, axis=0))
            terms = jnp.exp2((logits - top[None]) * (ROOT * math.log2(math.e)))
            w_ref[s, h] = terms
            total = spread_pairs(jnp.sum(terms, axis=0))
            inverse_ref[s, h] = 1.0 / total
            tops.append(top)
            totals.append(total)
        top = jnp.where(half == 0, tops[0], tops[1])
        total = jnp.where(half == 0, totals[0], totals[1])
        message = token_sum(top * ROOT + jnp.log(total), same) - log_len
        own_ref[s] = message
        msg_ref[s] = message[:CANDS]
        sall[s, s, y] = message[:CANDS]
        send_scores(s, s, 1).start()

        def ahead(t):
            for k in range(SIDES):
                send_scores(s, t, k).start()

        each(s + 1, WINDOW, ahead)

    def behind_block(s):
        def behind(t):
            for k in range(SIDES):
                send_scores(s, t, k).start()

        each(0, s, behind)

    def grad_block(s):
        for j in range(WINDOW):
            for k in range(SIDES):
                side = (y + k) % SIDES

                @pl.when((s != j) | (k > 0))
                def _():
                    remote(
                        msg_ref.at[0],
                        sall.at[s, j, side],
                        s_send.at[0],
                        s_recv.at[(s * WINDOW + j) * SIDES + side],
                        0,
                        side,
                        core,
                    ).wait_recv()

        tile = sall[s]
        top = jnp.max(jnp.max(tile, axis=(0, 1)), axis=0, keepdims=True)
        terms = jnp.sum(jnp.exp(tile - top[None, None]), axis=(0, 1))
        lse = top + jnp.log(jnp.sum(terms, axis=0, keepdims=True))
        lse = jnp.broadcast_to(lse, (8, BLK))
        lse_ref[s] = lse
        here = (pos == y * (CORES * PER) + row8 % (CORES * PER)) & (s == 0)
        coef = jnp.exp(own_ref[s] - lse) - jnp.where(here, 1.0, 0.0)
        turned = pltpu.roll(coef, 2, 0)
        q_blk = qall[s].reshape(BLK, DIM)
        rows = []
        dq = jnp.zeros((DIM, BLK), F32)
        for h in range(CORES):
            c = jnp.where(half == h, coef, turned)
            c = c * inverse_ref[s, h]
            rows.append((w_ref[s, h] * c[None]).reshape(ROWS, BLK).astype(BF16))
            dq = dq + jnp.dot(turned_p[h], rows[h], preferred_element_type=F32)
        gsend[s] = dq.T.astype(BF16).reshape(SIDES, OWN, DIM)
        send_grads(s, 1).start()

        @pl.when(s > 0)
        def _():
            send_grads(s, 0).start()

        for h in range(CORES):
            pgacc[h] += jnp.dot(rows[h], q_blk, preferred_element_type=F32)

    def run(low, high):
        each(low, high, score_block)
        each(low, high, behind_block)
        each(0, high - low, lambda i: grad_block(high - 1 - i))

    place_x = b % RING_X
    first_layer = b % LAYER < RING_X
    early = jnp.where(first_layer, place_x + 1, WINDOW)
    each(0, early, score_block)
    each(0, early, behind_block)
    for h in range(CORES):
        turned_p[h] = p_ref[h].astype(F32).T.astype(BF16)
    each(0, early, lambda i: grad_block(early - 1 - i))
    for x in range(WINDOW - 1):
        pl.when(first_layer & (place_x == x))(functools.partial(run, x + 1, WINDOW))

    pair_pg = remote(pgacc.at[other], pgrecv, pair_send.at[2], pair_recv.at[2], 0, y, other)
    pair_pg.start()

    found = jnp.zeros((CANDS, BLK), F32)
    for side in range(SIDES):
        here = pos[:CANDS] == side * CANDS + row8[:CANDS]
        found = found + jnp.where(here, sall[0, 0, side], 0.0)
    loss = lse_ref[0][0:1] - jnp.sum(found, axis=0, keepdims=True)
    one = [
        jnp.sum(jnp.where(lane8[0:1] == y * OWN + n * QTOK, loss, 0.0)) for n in range(PER)
    ]
    place = lax.broadcasted_iota(jnp.int32, (1, PER), 1)
    loss_ref[...] = jnp.where(place == 0, one[0], one[1])

    qg = gsend[0, y].astype(F32)
    for s in range(WINDOW):
        for k in range(SIDES):
            if s or k:
                i = s * SIDES + (y + k) % SIDES
                remote(
                    gsend.at[0, 0], grecv.at[i], g_send.at[0], g_recv.at[i], 0, y, core
                ).wait_recv()
                qg = qg + grecv[i].astype(F32)
    qg_ref[...] = qg * ROOT
    for s in range(WINDOW):
        for k in range(SIDES):
            if s or k:
                send_queries(s, k).wait_send()
            for t in range(WINDOW):
                if s != t or k:
                    send_scores(s, t, k).wait_send()
    pair_p.wait_send()
    pair_len.wait_send()
    pair_pg.wait_recv()
    pg_ref[...] = (pgacc[core] + pgrecv[...]) * ROOT

    pair_pg.wait_send()
    for s in range(WINDOW):
        for k in range(SIDES):
            if s or k:
                send_grads(s, k).wait_send()


def store(loss_ref, qg_ref, pg_ref, loss_out, qg_out, pg_out, sems):
    copies = [
        pltpu.make_async_copy(src, dst, sems.at[i])
        for i, (src, dst) in enumerate(
            ((pg_ref, pg_out), (qg_ref, qg_out), (loss_ref, loss_out))
        )
    ]
    for c in copies:
        c.start()
    for c in copies:
        c.wait()


def on_device(blocks, queries, passages, lengths, pos_index):
    hbm = pl.BlockSpec(memory_space=pltpu.HBM)
    vmem = pl.BlockSpec(memory_space=pltpu.VMEM)
    shapes = ((1, PER), (OWN, DIM), (ROWS, DIM))
    slots = WINDOW * SIDES
    dma = pltpu.SemaphoreType.DMA
    operands = (
        queries.reshape(OWN, DIM),
        passages.transpose(1, 0, 2).reshape(ROWS, DIM),
        lengths,
        pos_index,
    )
    results = pl.pallas_call(
        functools.partial(work, blocks),
        out_shape=tuple(pltpu.VMEM(s, F32) for s in shapes),
        in_specs=[hbm] * 4,
        out_specs=(vmem,) * 3,
        scratch_shapes=[
            pltpu.VMEM((WINDOW, SIDES, OWN, DIM), BF16),
            pltpu.VMEM((CORES, ROWS, DIM), BF16),
            pltpu.VMEM((WINDOW, CORES, TILES, 8, BLK), F32),
            pltpu.VMEM((WINDOW, 8, BLK), F32),
            pltpu.VMEM((WINDOW, CANDS, BLK), F32),
            pltpu.VMEM((WINDOW, WINDOW, SIDES, CANDS, BLK), F32),
            pltpu.VMEM((CORES, 8, BLK), F32),
            pltpu.VMEM((CORES, 8, BLK), jnp.int32),
            pltpu.VMEM((WINDOW, CORES, 8, BLK), F32),
            pltpu.VMEM((WINDOW, SIDES, OWN, DIM), BF16),
            pltpu.VMEM((slots, OWN, DIM), BF16),
            pltpu.VMEM((CORES, ROWS, DIM), F32),
            pltpu.VMEM((ROWS, DIM), F32),
            pltpu.VMEM((CORES, DIM, ROWS), BF16),
            pltpu.VMEM((WINDOW, 8, BLK), F32),
            pltpu.SMEM((PER,), jnp.int32),
            pltpu.SMEM((1, WINDOW * PER), jnp.int32),
            dma((slots,)),
            dma((slots,)),
            dma((WINDOW * slots,)),
            dma((WINDOW * slots,)),
            dma((slots,)),
            dma((slots,)),
            dma((3,)),
            dma((3,)),
            dma((4,)),
        ],
        compiler_params=pltpu.CompilerParams(
            collective_id=0, has_side_effects=True, vmem_limit_bytes=24 * 1024 * 1024
        ),
    )(*(pltpu.with_memory_space_constraint(x, pltpu.HBM) for x in operands))
    loss, qg, pg = pl.pallas_call(
        store,
        out_shape=tuple(pltpu.HBM(s, F32) for s in shapes),
        in_specs=[vmem] * 3,
        out_specs=(hbm,) * 3,
        scratch_shapes=[dma((3,))],
    )(*(pltpu.with_memory_space_constraint(x, pltpu.VMEM) for x in results))
    return (
        loss.reshape(PER),
        qg.reshape(PER, QTOK, DIM),
        pg.reshape(PTOK, PER, DIM).transpose(1, 0, 2),
    )


def solution(mesh):
    placed = (
        P(("blk", "mp"), None, None),
        P(("blk", "mp"), None, None),
        P(("blk", "mp")),
        P("blk", None),
    )
    return jax.shard_map(
        functools.partial(on_device, mesh.shape["blk"]),
        mesh=mesh,
        in_specs=placed,
        out_specs=(P(("blk", "mp")), P(("blk", "mp"), None, None), P(("blk", "mp"), None, None)),
        check_vma=False,
    )
```

```python
import functools
import math

import jax
import jax.numpy as jnp
from jax import lax
from jax.experimental import pallas as pl
from jax.experimental.pallas import tpu as pltpu
from jax.sharding import PartitionSpec as P

WINDOW = 4
SIDES = 2
CORES = 2
PER = 2
CANDS = CORES * PER
QTOK = 32
PTOK = 180
DIM = 128
ROWS = PER * PTOK
TILES = ROWS // 8
OWN = PER * QTOK
BLK = SIDES * OWN
RING_X = 4
LAYER = 32
NEG = -1e30
ROOT = DIM ** (-0.5)
MESH = pl.DeviceIdType.MESH
F32 = jnp.float32
BF16 = jnp.bfloat16


def spread_pairs(x):
    x = x + pltpu.roll(x, 4, 0)
    return x + pltpu.roll(x, 2, 0)


def max_pairs(x):
    x = jnp.maximum(x, pltpu.roll(x, 4, 0))
    return jnp.maximum(x, pltpu.roll(x, 2, 0))


def token_sum(x, same):
    hi = x.astype(BF16)
    rest = x - hi.astype(F32)
    mid = rest.astype(BF16)
    low = (rest - mid.astype(F32)).astype(BF16)
    pieces = jnp.concatenate([hi, mid, low], axis=1)
    return jnp.dot(pieces, same, preferred_element_type=F32)


def each(low, high, body):
    if isinstance(low, int) and isinstance(high, int):
        for i in range(low, high):
            body(i)
    else:
        lax.fori_loop(low, high, lambda i, _: body(i) or 0, 0)


def work(
    blocks,
    q_hbm,
    p_hbm,
    len_hbm,
    pos_hbm,
    loss_ref,
    qg_ref,
    pg_ref,
    qall,
    p_ref,
    w_ref,
    own_ref,
    msg_ref,
    sall,
    lens_ref,
    left_ref,
    inverse_ref,
    gsend,
    grecv,
    pgacc,
    pgsend,
    pgrecv,
    turned_p,
    lse_ref,
    len_ref,
    pos_ref,
    q_send,
    q_recv,
    s_send,
    s_recv,
    g_send,
    g_recv,
    pair_send,
    pair_recv,
    local,
):
    b = lax.axis_index("blk")
    m = lax.axis_index("mp")
    y = m // CORES
    core = m % CORES
    other = 1 - core

    def block(d):
        return lax.rem(b + (d + blocks), blocks)

    def remote(src, dst, send, recv, d, side, who):
        return pltpu.make_async_remote_copy(
            src_ref=src,
            dst_ref=dst,
            send_sem=send,
            recv_sem=recv,
            device_id={"blk": block(d), "mp": side * CORES + who},
            device_id_type=MESH,
        )

    def send_queries(s, k):
        side = (y + k) % SIDES
        return remote(
            qall.at[0, y], qall.at[s, y], q_send.at[s * SIDES + k], q_recv.at[s * SIDES + y], s, side, core
        )

    def send_scores(s, t, k):
        side = (y + k) % SIDES
        return remote(
            msg_ref.at[s],
            sall.at[t, s, y],
            s_send.at[(s * WINDOW + t) * SIDES + k],
            s_recv.at[(t * WINDOW + s) * SIDES + y],
            t - s,
            side,
            core,
        )

    def send_grads(s, k):
        side = (y + k) % SIDES
        return remote(
            gsend.at[s, side],
            grecv.at[s * SIDES + y],
            g_send.at[s * SIDES + k],
            g_recv.at[s * SIDES + y],
            -s,
            side,
            core,
        )

    barrier = pltpu.get_barrier_semaphore()
    pl.semaphore_signal(
        barrier, inc=1, device_id={"blk": b, "mp": y * CORES + other}, device_id_type=MESH
    )
    get_len = pltpu.make_async_copy(len_hbm, len_ref, local.at[0])
    get_len.start()
    get_pos = pltpu.make_async_copy(pos_hbm, pos_ref, local.at[1])
    get_pos.start()
    get_q = pltpu.make_async_copy(q_hbm, qall.at[0, y], local.at[2])
    get_q.start()
    get_p = pltpu.make_async_copy(p_hbm, p_ref.at[core], local.at[3])
    get_p.start()

    near = [(d, k) for d in (0, -1, -2, -3) for k in range(SIDES) if d or k]
    for d, k in near:
        pl.semaphore_signal(
            barrier,
            inc=1,
            device_id={"blk": block(d), "mp": (y + k) % SIDES * CORES + core},
            device_id_type=MESH,
        )
    pgacc[...] = jnp.zeros_like(pgacc)
    get_q.wait()
    pl.semaphore_wait(barrier, len(near) + 1)

    for i in range(WINDOW - 1):
        s = (WINDOW - 1 - b % RING_X + i) % (WINDOW - 1) + 1
        for k in range(SIDES):
            send_queries(s, k).start()
    send_queries(0, 1).start()
    get_p.wait()
    pair_p = remote(p_ref.at[core], p_ref.at[core], pair_send.at[0], pair_recv.at[0], 0, y, other)
    pair_p.start()

    row8 = lax.broadcasted_iota(jnp.int32, (8, BLK), 0)
    lane8 = lax.broadcasted_iota(jnp.int32, (8, BLK), 1)
    parity = row8 % 2
    half = row8 // 2 % 2
    get_len.wait()
    lens_ref[core] = jnp.where(parity == 0, len_ref[0], len_ref[1]).astype(F32)
    pair_len = remote(
        lens_ref.at[core], lens_ref.at[core], pair_send.at[1], pair_recv.at[1], 0, y, other
    )
    pair_len.start()
    get_pos.wait()
    query_of = lane8 // QTOK
    pos = jnp.zeros((8, BLK), jnp.int32)
    for side in range(SIDES):
        for i in range(PER):
            n = side * CORES * PER + core * PER + i
            pos = jnp.where(query_of == side * PER + i, pos_ref[0, n], pos)
    same = (
        lax.broadcasted_iota(jnp.int32, (BLK, BLK), 0) // QTOK
        == lax.broadcasted_iota(jnp.int32, (BLK, BLK), 1) // QTOK
    ).astype(F32).astype(BF16)
    same = jnp.concatenate([same] * 3, axis=0)
    first_token = lax.broadcasted_iota(jnp.int32, (TILES, 8, BLK), 0) * 4
    pair_p.wait_recv()
    pair_len.wait_recv()
    log_len = jnp.log(jnp.where(half == 0, lens_ref[0], lens_ref[1])) * QTOK
    for h in range(CORES):
        left_ref[h] = lens_ref[h].astype(jnp.int32) - row8 // 2

    def score_block(s):
        def arrived(side):
            remote(
                q_hbm, qall.at[s, side], q_send.at[0], q_recv.at[s * SIDES + side], 0, side, core
            ).wait_recv()

        arrived(1 - y)

        @pl.when(s > 0)
        def _():
            arrived(y)

        q_blk = qall[s].reshape(BLK, DIM)
        tops = []
        totals = []
        for h in range(CORES):
            logits = lax.dot_general(
                p_ref[h], q_blk, (((1,), (1,)), ((), ())), preferred_element_type=F32
            ).reshape(TILES, 8, BLK)
            logits = jnp.where(left_ref[h][None] > first_token, logits, NEG)
            top = max_pairs(jnp.max(logits, axis=0))
            terms = jnp.exp2((logits - top[None]) * (ROOT * math.log2(math.e)))
            w_ref[s, h] = terms
            total = spread_pairs(jnp.sum(terms, axis=0))
            inverse_ref[s, h] = 1.0 / total
            tops.append(top)
            totals.append(total)
        top = jnp.where(half == 0, tops[0], tops[1])
        total = jnp.where(half == 0, totals[0], totals[1])
        message = token_sum(top * ROOT + jnp.log(total), same) - log_len
        own_ref[s] = message
        msg_ref[s] = message[:CANDS]
        sall[s, s, y] = message[:CANDS]
        send_scores(s, s, 1).start()

        def ahead(t):
            for k in range(SIDES):
                send_scores(s, t, k).start()

        each(s + 1, WINDOW, ahead)

    def behind_block(s):
        def behind(t):
            for k in range(SIDES):
                send_scores(s, t, k).start()

        each(0, s, behind)

    def grad_block(s):
        for j in range(WINDOW):
            for k in range(SIDES):
                side = (y + k) % SIDES

                @pl.when((s != j) | (k > 0))
                def _():
                    remote(
                        msg_ref.at[0],
                        sall.at[s, j, side],
                        s_send.at[0],
                        s_recv.at[(s * WINDOW + j) * SIDES + side],
                        0,
                        side,
                        core,
                    ).wait_recv()

        tile = sall[s]
        top = jnp.max(jnp.max(tile, axis=(0, 1)), axis=0, keepdims=True)
        terms = jnp.sum(jnp.exp(tile - top[None, None]), axis=(0, 1))
        lse = top + jnp.log(jnp.sum(terms, axis=0, keepdims=True))
        lse = jnp.broadcast_to(lse, (8, BLK))
        lse_ref[s] = lse
        here = (pos == y * (CORES * PER) + row8 % (CORES * PER)) & (s == 0)
        coef = jnp.exp(own_ref[s] - lse) - jnp.where(here, 1.0, 0.0)
        turned = pltpu.roll(coef, 2, 0)
        q_blk = qall[s].reshape(BLK, DIM)
        rows = []
        dq = jnp.zeros((DIM, BLK), F32)
        for h in range(CORES):
            c = jnp.where(half == h, coef, turned)
            c = c * inverse_ref[s, h]
            rows.append((w_ref[s, h] * c[None]).reshape(ROWS, BLK).astype(BF16))
            dq = dq + jnp.dot(turned_p[h], rows[h], preferred_element_type=F32)
        gsend[s] = dq.T.astype(BF16).reshape(SIDES, OWN, DIM)
        send_grads(s, 1).start()

        @pl.when(s > 0)
        def _():
            send_grads(s, 0).start()

        for h in range(CORES):
            pgacc[h] += jnp.dot(rows[h], q_blk, preferred_element_type=F32)

    def run(low, high):
        each(low, high, score_block)
        each(low, high, behind_block)
        each(0, high - low, lambda i: grad_block(high - 1 - i))

    place_x = b % RING_X
    first_layer = b % LAYER < RING_X
    early = jnp.where(first_layer, place_x + 1, WINDOW)
    each(0, early, score_block)
    each(0, early, behind_block)
    for h in range(CORES):
        turned_p[h] = p_ref[h].astype(F32).T.astype(BF16)
    each(0, early, lambda i: grad_block(early - 1 - i))
    for x in range(WINDOW - 1):
        pl.when(first_layer & (place_x == x))(functools.partial(run, x + 1, WINDOW))

    pgsend[...] = pgacc[other].astype(BF16)
    pair_pg = remote(pgsend, pgrecv, pair_send.at[2], pair_recv.at[2], 0, y, other)
    pair_pg.start()

    found = jnp.zeros((CANDS, BLK), F32)
    for side in range(SIDES):
        here = pos[:CANDS] == side * CANDS + row8[:CANDS]
        found = found + jnp.where(here, sall[0, 0, side], 0.0)
    loss = lse_ref[0][0:1] - jnp.sum(found, axis=0, keepdims=True)
    one = [
        jnp.sum(jnp.where(lane8[0:1] == y * OWN + n * QTOK, loss, 0.0)) for n in range(PER)
    ]
    place = lax.broadcasted_iota(jnp.int32, (1, PER), 1)
    loss_ref[...] = jnp.where(place == 0, one[0], one[1])

    qg = gsend[0, y].astype(F32)
    for s in range(WINDOW):
        for k in range(SIDES):
            if s or k:
                i = s * SIDES + (y + k) % SIDES
                remote(
                    gsend.at[0, 0], grecv.at[i], g_send.at[0], g_recv.at[i], 0, y, core
                ).wait_recv()
                qg = qg + grecv[i].astype(F32)
    qg_ref[...] = qg * ROOT
    for s in range(WINDOW):
        for k in range(SIDES):
            if s or k:
                send_queries(s, k).wait_send()
            for t in range(WINDOW):
                if s != t or k:
                    send_scores(s, t, k).wait_send()
    pair_p.wait_send()
    pair_len.wait_send()
    pair_pg.wait_recv()
    pg_ref[...] = (pgacc[core] + pgrecv[...].astype(F32)) * ROOT

    pair_pg.wait_send()
    for s in range(WINDOW):
        for k in range(SIDES):
            if s or k:
                send_grads(s, k).wait_send()


def store(loss_ref, qg_ref, pg_ref, loss_out, qg_out, pg_out, sems):
    copies = [
        pltpu.make_async_copy(src, dst, sems.at[i])
        for i, (src, dst) in enumerate(
            ((pg_ref, pg_out), (qg_ref, qg_out), (loss_ref, loss_out))
        )
    ]
    for c in copies:
        c.start()
    for c in copies:
        c.wait()


def on_device(blocks, queries, passages, lengths, pos_index):
    hbm = pl.BlockSpec(memory_space=pltpu.HBM)
    vmem = pl.BlockSpec(memory_space=pltpu.VMEM)
    shapes = ((1, PER), (OWN, DIM), (ROWS, DIM))
    slots = WINDOW * SIDES
    dma = pltpu.SemaphoreType.DMA
    operands = (
        queries.reshape(OWN, DIM),
        passages.transpose(1, 0, 2).reshape(ROWS, DIM),
        lengths,
        pos_index,
    )
    results = pl.pallas_call(
        functools.partial(work, blocks),
        out_shape=tuple(pltpu.VMEM(s, F32) for s in shapes),
        in_specs=[hbm] * 4,
        out_specs=(vmem,) * 3,
        scratch_shapes=[
            pltpu.VMEM((WINDOW, SIDES, OWN, DIM), BF16),
            pltpu.VMEM((CORES, ROWS, DIM), BF16),
            pltpu.VMEM((WINDOW, CORES, TILES, 8, BLK), F32),
            pltpu.VMEM((WINDOW, 8, BLK), F32),
            pltpu.VMEM((WINDOW, CANDS, BLK), F32),
            pltpu.VMEM((WINDOW, WINDOW, SIDES, CANDS, BLK), F32),
            pltpu.VMEM((CORES, 8, BLK), F32),
            pltpu.VMEM((CORES, 8, BLK), jnp.int32),
            pltpu.VMEM((WINDOW, CORES, 8, BLK), F32),
            pltpu.VMEM((WINDOW, SIDES, OWN, DIM), BF16),
            pltpu.VMEM((slots, OWN, DIM), BF16),
            pltpu.VMEM((CORES, ROWS, DIM), F32),
            pltpu.VMEM((ROWS, DIM), BF16),
            pltpu.VMEM((ROWS, DIM), BF16),
            pltpu.VMEM((CORES, DIM, ROWS), BF16),
            pltpu.VMEM((WINDOW, 8, BLK), F32),
            pltpu.SMEM((PER,), jnp.int32),
            pltpu.SMEM((1, WINDOW * PER), jnp.int32),
            dma((slots,)),
            dma((slots,)),
            dma((WINDOW * slots,)),
            dma((WINDOW * slots,)),
            dma((slots,)),
            dma((slots,)),
            dma((3,)),
            dma((3,)),
            dma((4,)),
        ],
        compiler_params=pltpu.CompilerParams(
            collective_id=0, has_side_effects=True, vmem_limit_bytes=24 * 1024 * 1024
        ),
    )(*(pltpu.with_memory_space_constraint(x, pltpu.HBM) for x in operands))
    loss, qg, pg = pl.pallas_call(
        store,
        out_shape=tuple(pltpu.HBM(s, F32) for s in shapes),
        in_specs=[vmem] * 3,
        out_specs=(hbm,) * 3,
        scratch_shapes=[dma((3,))],
    )(*(pltpu.with_memory_space_constraint(x, pltpu.VMEM) for x in results))
    return (
        loss.reshape(PER),
        qg.reshape(PER, QTOK, DIM),
        pg.reshape(PTOK, PER, DIM).transpose(1, 0, 2),
    )


def solution(mesh):
    placed = (
        P(("blk", "mp"), None, None),
        P(("blk", "mp"), None, None),
        P(("blk", "mp")),
        P("blk", None),
    )
    return jax.shard_map(
        functools.partial(on_device, mesh.shape["blk"]),
        mesh=mesh,
        in_specs=placed,
        out_specs=(P(("blk", "mp")), P(("blk", "mp"), None, None), P(("blk", "mp"), None, None)),
        check_vma=False,
    )
```
